256 devices in a mesh: wide: 32 (over z, x), narrow: 8 (over y, core).
Axes of the slice: x: 4, y: 4, z: 8, core: 2. Of those that a mesh axis runs over, the one named last changes fastest.
Arguments:
- table: float32 [65536, 512], P('wide'), may hold values from -6 to 6
- accum: float32 [65536], P('wide'), may hold values from 0.1 to 4
- ids: int32 [32, 2048], P('wide', 'narrow'), may hold values from 0 to 65535, as said below
- lengths: int32 [32], P('wide'), may hold values from 1 to 2048, 40960 in all
- w_uvqk: bfloat16 [512, 2048], replicated, may hold values from -0.25 to 0.25
- w_out: bfloat16 [512, 512], replicated, may hold values from -0.25 to 0.25
- cotangent: bfloat16 [32, 2048, 512], P('wide', 'narrow'), may hold values from -6 to 6
Outputs:
- output: bfloat16 [32, 2048, 512], P('wide', 'narrow')
- new_table: float32 [65536, 512], P('wide')
- new_accum: float32 [65536], P('wide')
The draws below stay inside these ranges and needn't reach their ends.
Inputs may be any that keep to these rules, and one draw needn't show every extreme that they name: Row r belongs to owner r // 2048. Among the 256 slots that one device holds (aligned blocks by both axes), at most 16 ids belong to any one owner, and in every draw one owner gets exactly 16 from every device. Ids at slots past a sequence's length are present but unused. The lengths sum to 40960; the longest is exactly 2048.
All inputs are finite; a program needn't handle non-finite values. No bound on the sum of `lengths` on one device may be relied on, other than what follows from the above.
Results may differ from the reference program's by a relative error of at most 0.007.
Values may be sent and summed in bfloat16 or wider, within the bound.
A program may use at most 128 MiB of HBM per device.

```python
import math
import jax
import jax.numpy as jnp
import numpy as np
from jax import lax

D = 512
HEADS = 8
HD = 64
ROWS_DEV = 2048
LMAX = 2048
NSEQ = 32
TOK_DEV = 256
CAP = 16
ATT = 512
ROWS = 65536
TOTAL_LEN = 40960
N_WIDE = 32
N_NARROW = 8


def draw_ids(key, part):
    key = jax.random.fold_in(key, 7)
    hot_owner = jax.random.randint(jax.random.fold_in(key, 1), (), 0, N_WIDE)
    slot_total = N_WIDE * CAP
    block_total = N_WIDE * N_NARROW

    def make_block(block_key):
        slot_index = jnp.arange(slot_total, dtype=jnp.int32)
        random_scores = jax.random.randint(block_key, (slot_total,), 0, 1 << 18) * slot_total + slot_index
        random_scores = jnp.where(slot_index // CAP == hot_owner, -1 - slot_index, random_scores)
        ranking = jnp.argsort(random_scores)
        chosen = ranking[:TOK_DEV]
        chosen = jax.random.permutation(jax.random.fold_in(block_key, 2), chosen)
        owner_id = chosen // CAP
        local_row = jax.random.randint(jax.random.fold_in(block_key, 3), (TOK_DEV,), 0, ROWS_DEV)
        return owner_id * ROWS_DEV + local_row
    block_keys = jax.random.split(jax.random.fold_in(key, 2), block_total)
    id_table = jax.vmap(make_block)(block_keys)
    id_table = id_table.reshape(N_WIDE, N_NARROW, 1, TOK_DEV).transpose(0, 2, 1, 3).reshape(NSEQ, LMAX)
    return id_table.astype(jnp.int32)


def shard_levels(key, extent, shards, least, top_value):
    loudness, own = 1.0, jax.random.fold_in(key, 6)
    for position, shards_of in shards:
        steps = jnp.exp(jax.random.uniform(jax.random.fold_in(own, position), (shards_of,), jnp.float32, least / len(shards), top_value / len(shards)))
        loudness = loudness * jnp.repeat(steps, extent[position] // shards_of).reshape([-1 if axis == position else 1 for axis in range(len(extent))])
    return loudness


def length_profile(number_of, total, bound, slope):
    weights = [(1 << 20) // math.isqrt(standing ** slope) + 1 for standing in range(2, number_of + 1)]
    surplus, counts = total - bound - (number_of - 1), [1] * (number_of - 1)
    while surplus > 0:
        candidates = [i for i in range(number_of - 1) if counts[i] < bound]
        pool, budget = sum([weights[i] for i in candidates]), surplus
        for i in candidates:
            more = min(bound - counts[i], max(1, budget * weights[i] // pool), surplus)
            counts[i] = counts[i] + more
            surplus = surplus - more
    return np.array([bound] + counts)


def ragged_sizes(own_key, number_of, total, limit, skew):
    if number_of == 2:
        one = jax.random.randint(own_key, (), max(1, total - limit), min(limit, total - 1) + 1)
        return jnp.stack([one, total - one])
    sizes = jnp.asarray(length_profile(number_of, total, limit, skew), jnp.int32)
    pairs = (number_of - 1) // 2
    source_of, taker = sizes[1:1 + 2 * pairs:2], sizes[2:2 + 2 * pairs:2]
    margin = jnp.minimum(source_of - 1, limit - taker)
    moved = jax.random.randint(jax.random.fold_in(own_key, 1), (pairs,), 0, 1 << 20) % (margin + 1)
    sizes = sizes.at[1:1 + 2 * pairs:2].set(source_of - moved).at[2:2 + 2 * pairs:2].set(taker + moved)
    return sizes[jax.random.permutation(jax.random.fold_in(own_key, 2), number_of)]


def normal_values(rng, dims, width, bound, pieces=(), kind=jnp.bfloat16):
    level = shard_levels(rng, dims, pieces, -0.22, 0.18) if pieces else 1.0
    array = jax.random.normal(rng, dims, jnp.float32) * width * level
    return jnp.minimum(jnp.maximum(array, -bound), bound).astype(kind)


def setup_inputs(seed: int = 0) -> dict:
    arg_keys = jax.random.split(jax.random.key(seed), 8)
    return {
        "table": normal_values(arg_keys[0], (ROWS, D), 1.0, 6.0, ((0, 32),), jnp.float32),
        "accum": jnp.clip(jnp.exp(math.log(4.0) - 3.6888794 * jax.random.uniform(arg_keys[1], (ROWS,), jnp.float32) ** shard_levels(arg_keys[1], (ROWS,), ((0, 32),), -0.2, 0.2)), 0.1, 4.0),
        "ids": draw_ids(jax.random.fold_in(arg_keys[7], 71), 0),
        "lengths": ragged_sizes(arg_keys[3], NSEQ, TOTAL_LEN, LMAX, 2).astype(jnp.int32),
        "w_uvqk": normal_values(arg_keys[4], (D, 4 * ATT), D ** -0.5, 0.25),
        "w_out": normal_values(arg_keys[5], (ATT, D), ATT ** -0.5, 0.25),
        "cotangent": normal_values(arg_keys[6], (NSEQ, LMAX, D), 1.0, 6.0, ((0, 32), (1, 8))),
    }


norm_eps = 1e-05
learning_rate = 0.5

def silu_slope(value):
    sigma = jax.nn.sigmoid(value)
    return sigma * (1.0 + value * (1.0 - sigma))

def layer_norm(value):
    center = value - lax.optimization_barrier(jnp.mean(value, axis=-1, keepdims=True))
    inverse = lax.rsqrt(lax.optimization_barrier(jnp.mean(center * center, axis=-1, keepdims=True)) + norm_eps)
    return (center * inverse, inverse)

def norm_backward(grad, normed, inverse):
    return inverse * (grad - lax.optimization_barrier(jnp.mean(grad, axis=-1, keepdims=True)) - normed * lax.optimization_barrier(jnp.mean(grad * normed, axis=-1, keepdims=True)))

def reference(table, accum, ids, lengths, w_uvqk, w_out, cotangent):
    positions = jnp.arange(LMAX, dtype=jnp.int32)
    scale = 1.0 / math.sqrt(HD)
    part_index = jnp.arange(3, dtype=jnp.int32)[None, None, :, None]

    def one_sequence(operands):
        seq_ids, seq_len, seq_cot = operands
        embed = table[seq_ids].astype(jnp.bfloat16)
        live = positions < seq_len
        embed_f = embed.astype(jnp.float32)
        normed1, inverse1 = layer_norm(embed_f)
        hidden = jnp.dot(normed1.astype(jnp.bfloat16), w_uvqk, preferred_element_type=jnp.float32)
        hidden_u = hidden[:, :ATT]
        hidden_rest = hidden[:, ATT:].reshape(LMAX, HEADS, 3, HD)
        act_u = jax.nn.silu(hidden_u).astype(jnp.bfloat16)
        act_rest = jnp.where(part_index == 0, hidden_rest, jax.nn.silu(hidden_rest)).astype(jnp.bfloat16)
        values = act_rest[:, :, 0].astype(jnp.float32)
        queries = act_rest[:, :, 1].astype(jnp.float32)
        keys_all = act_rest[:, :, 2].astype(jnp.float32)
        mask = (positions[None, :] <= positions[:, None]) & live[:, None]
        scores = jnp.einsum('ihd,jhd->hij', queries, keys_all) * scale
        weights = jnp.where(mask[None], jax.nn.silu(scores), 0.0).astype(jnp.bfloat16)
        attended = jnp.einsum('hij,jhd->ihd', weights.astype(jnp.float32), values).astype(jnp.bfloat16)
        normed2, inverse2 = layer_norm(attended.reshape(LMAX, ATT).astype(jnp.float32))
        act_u_f = act_u.astype(jnp.float32)
        mixed = (normed2 * act_u_f).astype(jnp.bfloat16)
        result = embed_f + jnp.dot(mixed, w_out, preferred_element_type=jnp.float32)
        result = jnp.where(live[:, None], result, 0.0).astype(jnp.bfloat16)
        upstream = jnp.where(live[:, None], seq_cot, jnp.zeros((), jnp.bfloat16))
        grad_mixed = jnp.dot(upstream, w_out.T, preferred_element_type=jnp.float32)
        grad_norm2 = grad_mixed * act_u_f
        grad_u = grad_mixed * normed2
        grad_attended = norm_backward(grad_norm2, normed2, inverse2).astype(jnp.bfloat16).reshape(LMAX, HEADS, HD)
        grad_att_f = grad_attended.astype(jnp.float32)
        grad_weights = jnp.einsum('ihd,jhd->hij', grad_att_f, values)
        grad_scores = jnp.where(mask[None], grad_weights * silu_slope(scores), 0.0).astype(jnp.bfloat16)
        grad_scores_f = grad_scores.astype(jnp.float32)
        grad_values = jnp.einsum('hij,ihd->jhd', weights.astype(jnp.float32), grad_att_f).astype(jnp.bfloat16)
        grad_queries = (jnp.einsum('hij,jhd->ihd', grad_scores_f, keys_all) * scale).astype(jnp.bfloat16)
        grad_keys = (jnp.einsum('hij,ihd->jhd', grad_scores_f, queries) * scale).astype(jnp.bfloat16)
        returned = jnp.stack([grad_values, grad_queries, grad_keys], axis=2).astype(jnp.float32)
        grad_rest = jnp.where(part_index == 0, returned, returned * silu_slope(hidden_rest)).reshape(LMAX, 3 * ATT)
        grad_hidden = jnp.concatenate([grad_u * silu_slope(hidden_u), grad_rest], axis=1).astype(jnp.bfloat16)
        grad_norm1 = jnp.dot(grad_hidden, w_uvqk.T, preferred_element_type=jnp.float32)
        grad_embed = norm_backward(grad_norm1, normed1, inverse1) + upstream.astype(jnp.float32)
        grad_embed = jnp.where(live[:, None], grad_embed, 0.0)
        return (result, grad_embed)
    output, grad_embed = lax.map(one_sequence, (ids, lengths, cotangent))
    block_ids = ids.reshape(NSEQ, N_NARROW, TOK_DEV)
    block_grads = grad_embed.reshape(NSEQ, N_NARROW, TOK_DEV, D)
    row_grad = jnp.zeros((ROWS, D), jnp.float32)
    for narrow_index in range(N_NARROW):
        partial_value = jnp.zeros((ROWS, D), jnp.float32).at[block_ids[:, narrow_index].reshape(-1)].add(block_grads[:, narrow_index].reshape(-1, D))
        row_grad = row_grad + lax.optimization_barrier(partial_value.astype(jnp.bfloat16)).astype(jnp.float32)
    new_accum = accum + lax.optimization_barrier(jnp.mean(row_grad * row_grad, axis=1))
    new_table = table - learning_rate * row_grad / jnp.sqrt(new_accum)[:, None]
    return (output, new_table, new_accum)
```

```python
import functools

import jax
import jax.numpy as jnp
from jax import lax
from jax.experimental import pallas as pl
from jax.experimental.pallas import tpu as pltpu
from jax.sharding import PartitionSpec as P

HEADS = 8
HD = 64
CAP = 16
EPS = 1e-05
RATE = 0.5
MESH = pl.DeviceIdType.MESH
F32 = jnp.float32
BF16 = jnp.bfloat16
MIB = 1 << 20

NN = (((1,), (0,)), ((), ()))
NT = (((1,), (1,)), ((), ()))
TN = (((0,), (0,)), ((), ()))


def mm(a, b, dims=NN):
    return lax.dot_general(a, b, dims, preferred_element_type=F32)


def iota(shape, dim):
    return lax.broadcasted_iota(jnp.int32, shape, dim)


def sigmoid(t):
    return 0.5 * jnp.tanh(0.5 * t) + 0.5


def silu(t):
    return t * sigmoid(t)


def silu_slope(t):
    s = sigmoid(t)
    return s * (1.0 + t * (1.0 - s))


def greet(axis, me, n):
    barrier = pltpu.get_barrier_semaphore()

    def one(k, carry):
        pl.semaphore_signal(
            barrier, inc=1, device_id={axis: lax.rem(me + k, n)}, device_id_type=MESH
        )
        return carry

    lax.fori_loop(1, n, one, 0)
    return lambda: pl.semaphore_wait(barrier, n - 1)


def remote(src, dst, send_sem, recv_sem, axis, peer):
    return pltpu.make_async_remote_copy(
        src_ref=src,
        dst_ref=dst,
        send_sem=send_sem,
        recv_sem=recv_sem,
        device_id={axis: peer},
        device_id_type=MESH,
    )


def fetch_kernel(
    n, table_ref, ids_ref, emb_ref, target_ref, lanes_ref,
    tab, tabb, asks, asked, picks, reply, replies, tab_sem, ss, rs, ss2, rs2,
):
    me = lax.axis_index("wide")
    greeted = greet("wide", me, n)
    rows_dev = table_ref.shape[0]
    tokens = ids_ref.shape[1]
    load = pltpu.make_async_copy(table_ref, tab, tab_sem)
    load.start()

    ids = ids_ref[...]
    owner = ids // rows_dev
    row = ids - owner * rows_dev
    hits = owner == iota((n, tokens), 0)
    hits_f = hits.astype(F32)
    before = (iota((tokens, tokens), 0) < iota((tokens, tokens), 1)).astype(F32).astype(BF16)
    earlier = mm(hits_f.astype(BF16), before)
    slot = jnp.sum(earlier * hits_f, axis=0, keepdims=True).astype(jnp.int32)
    target = owner * CAP + slot
    target_ref[...] = target
    place = slot + CAP * lax.rem(me, 8)
    at_place = (place == iota((128, tokens), 0)).astype(F32).astype(BF16)
    high = row // 256
    low = row - high * 256
    high_m = (hits_f * high.astype(F32)).astype(BF16)
    low_m = (hits_f * low.astype(F32)).astype(BF16)
    wanted = (mm(high_m, at_place, NT) * 256.0 + mm(low_m, at_place, NT)).astype(jnp.int32)
    for o in range(n):
        asks[o] = wanted[o : o + 1, :]

    greeted()

    def ask(k):
        peer = lax.rem(me + k, n)
        return remote(asks.at[peer], asked.at[me], ss.at[k], rs.at[k], "wide", peer)

    lax.fori_loop(1, n, lambda k, c: (ask(k).start(), c)[1], 0)
    asked[me] = asks[me]
    load.wait()
    tabb[...] = tab[...].astype(BF16)
    lax.fori_loop(1, n, lambda k, c: (ask(k).wait_recv(), c)[1], 0)

    lane16 = iota((CAP, 128), 1)
    sub16 = iota((CAP, 128), 0)
    row_iota = iota((CAP, rows_dev), 1)
    for k in range(n):
        peer = lax.rem(me + k, n)
        line = jnp.broadcast_to(asked[peer], (CAP, 128)).astype(F32)
        mine = lane16 == sub16 + CAP * lax.rem(peer, 8)
        column = jnp.sum(jnp.where(mine, line, 0.0), axis=1, keepdims=True).astype(jnp.int32)
        picks[CAP * k : CAP * (k + 1), :] = (column == row_iota).astype(F32).astype(BF16)
    for g in range(n // 8):
        total = asked[8 * g]
        for j in range(1, 8):
            total = total + asked[8 * g + j]
        lanes_ref[g : g + 1, :] = total
    if n // 8 < 8:
        lanes_ref[n // 8 :, :] = jnp.zeros((8 - n // 8, 128), jnp.int32)

    def answer(k):
        peer = lax.rem(me + k, n)
        return remote(
            reply.at[pl.ds(pl.multiple_of(k * CAP, CAP), CAP)],
            replies.at[pl.ds(pl.multiple_of(me * CAP, CAP), CAP)],
            ss2.at[k],
            rs2.at[k],
            "wide",
            peer,
        )

    half = n // 2
    for part in range(2):
        lo = part * half * CAP
        reply[lo : lo + half * CAP, :] = mm(picks[lo : lo + half * CAP, :], tabb[...]).astype(BF16)
        lax.fori_loop(
            max(1, part * half), (part + 1) * half, lambda k, c: (answer(k).start(), c)[1], 0
        )
    replies[pl.ds(pl.multiple_of(me * CAP, CAP), CAP), :] = reply[:CAP, :]

    target_t = jnp.transpose(jnp.broadcast_to(target.astype(F32), (128, tokens))).astype(jnp.int32)
    take = jnp.concatenate(
        [
            (target_t == iota((tokens, 128), 1) + 128 * g).astype(F32).astype(BF16)
            for g in range(n * CAP // 128)
        ],
        axis=1,
    )
    lax.fori_loop(1, n, lambda k, c: (answer(k).wait_recv(), c)[1], 0)
    emb_ref[...] = mm(take, replies[...]).astype(BF16)

    def done(k, c):
        ask(k).wait_send()
        answer(k).wait_send()
        return c

    lax.fori_loop(1, n, done, 0)


def fetch(n, table, ids):
    rows_dev, width = table.shape
    tokens = ids.shape[1]
    vmem = pl.BlockSpec(memory_space=pltpu.VMEM)
    return pl.pallas_call(
        functools.partial(fetch_kernel, n),
        out_shape=(
            jax.ShapeDtypeStruct((tokens, width), BF16),
            jax.ShapeDtypeStruct((1, tokens), jnp.int32),
            jax.ShapeDtypeStruct((8, 128), jnp.int32),
        ),
        in_specs=[pl.BlockSpec(memory_space=pl.ANY), vmem],
        out_specs=(vmem, vmem, vmem),
        scratch_shapes=[
            pltpu.VMEM((rows_dev, width), F32),
            pltpu.VMEM((rows_dev, width), BF16),
            pltpu.VMEM((n, 1, 128), jnp.int32),
            pltpu.VMEM((n, 1, 128), jnp.int32),
            pltpu.VMEM((n * CAP, rows_dev), BF16),
            pltpu.VMEM((n * CAP, width), BF16),
            pltpu.VMEM((n * CAP, width), BF16),
            pltpu.SemaphoreType.DMA,
            pltpu.SemaphoreType.DMA((n,)),
            pltpu.SemaphoreType.DMA((n,)),
            pltpu.SemaphoreType.DMA((n,)),
            pltpu.SemaphoreType.DMA((n,)),
        ],
        compiler_params=pltpu.CompilerParams(
            collective_id=0, has_side_effects=True, vmem_limit_bytes=32 * MIB
        ),
    )(table, ids)


def norm_back(grad, normed, inverse):
    return inverse * (
        grad
        - jnp.mean(grad, axis=0, keepdims=True)
        - normed * jnp.mean(grad * normed, axis=0, keepdims=True)
    )


def layer_kernel(
    n, emb_ref, len_ref, w_ref, wo_ref, cot_ref, out_ref, ge_ref,
    hid, normed1, qkv_out, qkv, keys, vals, wts, slopes, heads_out, heads, gm, gu,
    gatt_out, gatt, dq, back_out, back, gh, ss, rs,
):
    me = lax.axis_index("narrow")
    greeted = greet("narrow", me, n)
    tokens, width = emb_ref.shape
    att = HEADS * HD
    length = len_ref[0]

    def exchange(step, source, landing, peer):
        return remote(
            source.at[peer], landing.at[me], ss.at[step, peer], rs.at[step, me], "narrow", peer
        )

    def arrived(step, source, landing, peer):
        return pltpu.make_async_remote_copy(
            src_ref=source.at[peer],
            dst_ref=landing.at[peer],
            send_sem=ss.at[step, peer],
            recv_sem=rs.at[step, peer],
            device_id={"narrow": peer},
            device_id_type=MESH,
        )

    def wait_all(step, source, landing):
        def one(k, c):
            arrived(step, source, landing, lax.rem(me + k, n)).wait_recv()
            return c

        lax.fori_loop(1, n, one, 0)

    emb_t = jnp.transpose(emb_ref[...].astype(F32))
    center = emb_t - jnp.mean(emb_t, axis=0, keepdims=True)
    inverse1 = lax.rsqrt(jnp.mean(center * center, axis=0, keepdims=True) + EPS)
    normed = center * inverse1
    normed1[...] = normed
    normed_b = normed.astype(BF16)
    chunk = 256
    total = w_ref.shape[1]
    for c in range(att // chunk, total // chunk):
        hid[c * chunk : (c + 1) * chunk, :] = mm(w_ref[:, c * chunk : (c + 1) * chunk], normed_b, TN)
    greeted()

    def send_head(k, carry):
        peer = lax.rem(me + k, n)
        base = pl.multiple_of(att + 3 * HD * peer, HD)
        qkv_out[peer, :HD, :] = hid[pl.ds(base, HD), :].astype(BF16)
        qkv_out[peer, HD:, :] = silu(hid[pl.ds(base + HD, 2 * HD), :]).astype(BF16)
        exchange(0, qkv_out, qkv, peer).start()
        return carry

    lax.fori_loop(1, n, send_head, 0)
    base = pl.multiple_of(att + 3 * HD * me, HD)
    qkv[me, :HD, :] = hid[pl.ds(base, HD), :].astype(BF16)
    qkv[me, HD:, :] = silu(hid[pl.ds(base + HD, 2 * HD), :]).astype(BF16)

    for c in range(att // chunk):
        hid[c * chunk : (c + 1) * chunk, :] = mm(w_ref[:, c * chunk : (c + 1) * chunk], normed_b, TN)
    live = iota((tokens, 1), 0) + me * tokens < length
    upstream = jnp.where(live, cot_ref[...], jnp.zeros((), BF16))
    gm[...] = mm(wo_ref[...], upstream, NT)
    wait_all(0, qkv_out, qkv)

    scale = HD**-0.5
    for b in range(n):
        vals[b] = jnp.transpose(qkv[b, :HD, :].astype(F32)).astype(BF16)
        keys[b] = jnp.transpose(qkv[b, 2 * HD :, :].astype(F32)).astype(BF16)
    causal = iota((tokens, tokens), 0) <= iota((tokens, tokens), 1)
    for i in range(n):
        query = qkv[i, HD : 2 * HD, :] * scale
        attended = jnp.zeros((HD, tokens), F32)
        for j in range(i + 1):
            scores = mm(keys[j], query)
            s = sigmoid(scores)
            weight = scores * s
            slope = s + weight * (1.0 - s)
            if i == j:
                weight = jnp.where(causal, weight, 0.0)
                slope = jnp.where(causal, slope, 0.0)
            weight = weight.astype(BF16)
            wts[j, i] = weight
            slopes[j, i] = slope.astype(BF16)
            attended = attended + mm(qkv[j, :HD, :], weight)
        heads_out[i] = attended.astype(BF16)

        @pl.when(i != me)
        def _():
            exchange(1, heads_out, heads, i).start()

        @pl.when(i == me)
        def _():
            heads[i] = heads_out[i]

    wait_all(1, heads_out, heads)

    merged = heads[...].astype(F32).reshape(att, tokens)
    center = merged - jnp.mean(merged, axis=0, keepdims=True)
    inverse2 = lax.rsqrt(jnp.mean(center * center, axis=0, keepdims=True) + EPS)
    normed2 = center * inverse2
    gate = silu(hid[:att, :]).astype(BF16).astype(F32)
    grad_mixed = gm[...]
    gu[...] = grad_mixed * normed2
    grad_att = norm_back(grad_mixed * gate, normed2, inverse2).astype(BF16)
    gatt_out[...] = grad_att.reshape(n, HD, tokens)

    def send_grad(k, carry):
        exchange(2, gatt_out, gatt, lax.rem(me + k, n)).start()
        return carry

    lax.fori_loop(1, n, send_grad, 0)
    gatt[me] = gatt_out[me]
    mixed = jnp.transpose(normed2 * gate).astype(BF16)
    result = emb_ref[...].astype(F32) + mm(mixed, wo_ref[...])
    out_ref[...] = jnp.where(live, result, 0.0).astype(BF16)
    wait_all(2, gatt_out, gatt)

    dq[...] = jnp.zeros_like(dq)
    for j in range(n):
        dv = jnp.zeros((HD, tokens), F32)
        dk = jnp.zeros((HD, tokens), F32)
        for i in range(j, n):
            grad = gatt[i]
            dw = mm(vals[j], grad)
            ds = (dw * slopes[j, i].astype(F32)).astype(BF16)
            dv = dv + mm(grad, wts[j, i], NT)
            dk = dk + mm(qkv[i, HD : 2 * HD, :], ds, NT)
            dq[i] += mm(qkv[j, 2 * HD :, :], ds)
        back_out[j, :HD, :] = dv.astype(BF16)
        back_out[j, HD : 2 * HD, :] = (dq[j] * scale).astype(BF16)
        back_out[j, 2 * HD :, :] = (dk * scale).astype(BF16)

        @pl.when(j != me)
        def _():
            exchange(3, back_out, back, j).start()

        @pl.when(j == me)
        def _():
            back[j] = back_out[j]

    gh[:att, :] = (gu[...] * silu_slope(hid[:att, :])).astype(BF16)
    upstream_t = jnp.transpose(upstream.astype(F32))
    wait_all(3, back_out, back)
    for h in range(HEADS):
        base = att + 3 * HD * h
        gh[base : base + HD, :] = back[h, :HD, :]
        gh[base + HD : base + 3 * HD, :] = (
            back[h, HD:, :].astype(F32) * silu_slope(hid[base + HD : base + 3 * HD, :])
        ).astype(BF16)
    grad_norm1 = mm(w_ref[...], gh[...])
    grad_emb = norm_back(grad_norm1, normed1[...], inverse1) + upstream_t
    live_t = iota((1, tokens), 1) + me * tokens < length
    ge_ref[...] = jnp.where(live_t, grad_emb, 0.0).astype(BF16)

    def done(k, c):
        peer = lax.rem(me + k, n)
        arrived(0, qkv_out, qkv, peer).wait_send()
        arrived(1, heads_out, heads, peer).wait_send()
        arrived(2, gatt_out, gatt, peer).wait_send()
        arrived(3, back_out, back, peer).wait_send()
        return c

    lax.fori_loop(1, n, done, 0)


def layer(n, emb, lengths, w_uvqk, w_out, cotangent):
    tokens, width = emb.shape
    att = HEADS * HD
    vmem = pl.BlockSpec(memory_space=pltpu.VMEM)
    return pl.pallas_call(
        functools.partial(layer_kernel, n),
        out_shape=(
            jax.ShapeDtypeStruct((tokens, width), BF16),
            jax.ShapeDtypeStruct((width, tokens), BF16),
        ),
        in_specs=[vmem, pl.BlockSpec(memory_space=pltpu.SMEM), vmem, vmem, vmem],
        out_specs=(vmem, vmem),
        scratch_shapes=[
            pltpu.VMEM((4 * att, tokens), F32),
            pltpu.VMEM((width, tokens), F32),
            pltpu.VMEM((n, 3 * HD, tokens), BF16),
            pltpu.VMEM((n, 3 * HD, tokens), BF16),
            pltpu.VMEM((n, tokens, HD), BF16),
            pltpu.VMEM((n, tokens, HD), BF16),
            pltpu.VMEM((n, n, tokens, tokens), BF16),
            pltpu.VMEM((n, n, tokens, tokens), BF16),
            pltpu.VMEM((n, HD, tokens), BF16),
            pltpu.VMEM((n, HD, tokens), BF16),
            pltpu.VMEM((att, tokens), F32),
            pltpu.VMEM((att, tokens), F32),
            pltpu.VMEM((n, HD, tokens), BF16),
            pltpu.VMEM((n, HD, tokens), BF16),
            pltpu.VMEM((n, HD, tokens), F32),
            pltpu.VMEM((n, 3 * HD, tokens), BF16),
            pltpu.VMEM((n, 3 * HD, tokens), BF16),
            pltpu.VMEM((4 * att, tokens), BF16),
            pltpu.SemaphoreType.DMA((4, n)),
            pltpu.SemaphoreType.DMA((4, n)),
        ],
        compiler_params=pltpu.CompilerParams(
            collective_id=1, has_side_effects=True, vmem_limit_bytes=48 * MIB
        ),
    )(emb, lengths, w_uvqk, w_out, cotangent)


def scatter_kernel(
    n, ge_ref, target_ref, lanes_ref, part_ref, outgoing, arriving, hot, ss, rs
):
    me = lax.axis_index("wide")
    greeted = greet("wide", me, n)
    rows_dev = part_ref.shape[0]
    tokens = ge_ref.shape[1]
    slots = n * CAP
    put = (iota((slots, tokens), 0) == target_ref[...]).astype(F32).astype(BF16)
    outgoing[...] = mm(put, ge_ref[...], NT).astype(BF16)
    greeted()

    def give(k):
        peer = lax.rem(me + k, n)
        return remote(
            outgoing.at[pl.ds(pl.multiple_of(peer * CAP, CAP), CAP)],
            arriving.at[pl.ds(pl.multiple_of(me * CAP, CAP), CAP)],
            ss.at[k],
            rs.at[k],
            "wide",
            peer,
        )

    lax.fori_loop(1, n, lambda k, c: (give(k).start(), c)[1], 0)
    own = pl.ds(pl.multiple_of(me * CAP, CAP), CAP)
    arriving[own, :] = outgoing[own, :]
    for g in range(slots // 128):
        hot[:, 128 * g : 128 * (g + 1)] = (
            (iota((rows_dev, 128), 0) == lanes_ref[g : g + 1, :]).astype(F32).astype(BF16)
        )
    lax.fori_loop(1, n, lambda k, c: (give(k).wait_recv(), c)[1], 0)
    part_ref[...] = mm(hot[...], arriving[...]).astype(BF16)
    lax.fori_loop(1, n, lambda k, c: (give(k).wait_send(), c)[1], 0)


def scatter(n, rows_dev, grad_emb, target, lanes):
    width, tokens = grad_emb.shape
    vmem = pl.BlockSpec(memory_space=pltpu.VMEM)
    return pl.pallas_call(
        functools.partial(scatter_kernel, n),
        out_shape=jax.ShapeDtypeStruct((rows_dev, width), BF16),
        in_specs=[vmem, vmem, vmem],
        out_specs=vmem,
        scratch_shapes=[
            pltpu.VMEM((n * CAP, width), BF16),
            pltpu.VMEM((n * CAP, width), BF16),
            pltpu.VMEM((rows_dev, n * CAP), BF16),
            pltpu.SemaphoreType.DMA((n,)),
            pltpu.SemaphoreType.DMA((n,)),
        ],
        compiler_params=pltpu.CompilerParams(
            collective_id=2, has_side_effects=True, vmem_limit_bytes=32 * MIB
        ),
    )(grad_emb, target, lanes)


def sum_kernel(n, part_ref, sum_ref, sib_in, half_sum, blocks_in, ss, rs):
    me = lax.axis_index("narrow")
    greeted = greet("narrow", me, n)
    chip = me // 2
    core = lax.rem(me, 2)
    sibling = chip * 2 + 1 - core
    chips = n // 2
    rows_dev, width = part_ref.shape
    half = rows_dev // 2
    block = half // chips
    greeted()

    def rows(ref, start, size):
        return ref.at[pl.ds(pl.multiple_of(start, block), size)]

    swap = remote(
        rows(part_ref, (1 - core) * half, half), sib_in, ss.at[0], rs.at[0], "narrow", sibling
    )
    swap.start()
    swap.wait_recv()
    half_sum[...] = (
        part_ref[pl.ds(pl.multiple_of(core * half, block), half), :].astype(F32)
        + sib_in[...].astype(F32)
    ).astype(BF16)

    def spread(k):
        other = lax.rem(chip + k, chips)
        return remote(
            rows(half_sum, other * block, block),
            blocks_in.at[k],
            ss.at[k],
            rs.at[k],
            "narrow",
            other * 2 + core,
        )

    for k in range(1, chips):
        spread(k).start()
    total = half_sum[pl.ds(pl.multiple_of(chip * block, block), block), :].astype(F32)
    for k in range(1, chips):
        spread(k).wait_recv()
        total = total + blocks_in[k].astype(F32)
    mine = core * half + chip * block
    sum_ref[pl.ds(pl.multiple_of(mine, block), block), :] = total.astype(BF16)

    def collect(k):
        other = lax.rem(chip + k, chips)
        return remote(
            rows(sum_ref, mine, block),
            rows(sum_ref, mine, block),
            ss.at[chips + k],
            rs.at[chips + k],
            "narrow",
            other * 2 + core,
        )

    def pass_on(k):
        source = lax.rem(chip + chips - k, chips)
        start = core * half + source * block
        return remote(
            rows(sum_ref, start, block),
            rows(sum_ref, start, block),
            ss.at[2 * chips + k],
            rs.at[2 * chips + k],
            "narrow",
            sibling,
        )

    for k in range(1, chips):
        collect(k).start()
    pass_on(0).start()
    for k in range(1, chips):
        collect(k).wait_recv()
        pass_on(k).start()
    for k in range(chips):
        pass_on(k).wait_recv()
    swap.wait_send()
    for k in range(1, chips):
        spread(k).wait_send()
        collect(k).wait_send()
    for k in range(chips):
        pass_on(k).wait_send()


def sum_rows(n, partial):
    rows_dev, width = partial.shape
    vmem = pl.BlockSpec(memory_space=pltpu.VMEM)
    half = rows_dev // 2
    chips = n // 2
    return pl.pallas_call(
        functools.partial(sum_kernel, n),
        out_shape=jax.ShapeDtypeStruct((rows_dev, width), BF16),
        in_specs=[vmem],
        out_specs=vmem,
        scratch_shapes=[
            pltpu.VMEM((half, width), BF16),
            pltpu.VMEM((half, width), BF16),
            pltpu.VMEM((chips, half // chips, width), BF16),
            pltpu.SemaphoreType.DMA((3 * chips,)),
            pltpu.SemaphoreType.DMA((3 * chips,)),
        ],
        compiler_params=pltpu.CompilerParams(
            collective_id=3, has_side_effects=True, vmem_limit_bytes=32 * MIB
        ),
    )(partial)


def local(table, accum, ids, lengths, w_uvqk, w_out, cotangent):
    n_wide = lax.axis_size("wide")
    n_narrow = lax.axis_size("narrow")
    rows_dev, width = table.shape
    tokens = ids.shape[1]
    emb, target, lanes = fetch(n_wide, table, ids)
    output, grad_emb = layer(
        n_narrow, emb, lengths, w_uvqk, w_out, cotangent.reshape(tokens, width)
    )
    partial = scatter(n_wide, rows_dev, grad_emb, target, lanes)
    summed = sum_rows(n_narrow, partial).astype(F32)
    new_accum = accum + jnp.mean(summed * summed, axis=1)
    new_table = table - RATE * summed / jnp.sqrt(new_accum)[:, None]
    return (output.reshape(1, tokens, width), new_table, new_accum)


def solution(mesh):
    in_specs = (
        P("wide", None),
        P("wide"),
        P("wide", "narrow"),
        P("wide"),
        P(),
        P(),
        P("wide", "narrow", None),
    )
    out_specs = (P("wide", "narrow", None), P("wide", None), P("wide"))
    return jax.shard_map(local, mesh=mesh, in_specs=in_specs, out_specs=out_specs, check_vma=False)
```

```python
import functools

import jax
import jax.numpy as jnp
from jax import lax
from jax.experimental import pallas as pl
from jax.experimental.pallas import tpu as pltpu
from jax.sharding import PartitionSpec as P

HEADS = 8
HD = 64
CAP = 16
EPS = 1e-05
RATE = 0.5
MESH = pl.DeviceIdType.MESH
F32 = jnp.float32
BF16 = jnp.bfloat16
MIB = 1 << 20

NN = (((1,), (0,)), ((), ()))
NT = (((1,), (1,)), ((), ()))
TN = (((0,), (0,)), ((), ()))


def mm(a, b, dims=NN):
    return lax.dot_general(a, b, dims, preferred_element_type=F32)


def iota(shape, dim):
    return lax.broadcasted_iota(jnp.int32, shape, dim)


def sigmoid(t):
    return 0.5 * jnp.tanh(0.5 * t) + 0.5


def silu(t):
    return t * sigmoid(t)


def silu_slope(t):
    s = sigmoid(t)
    return s * (1.0 + t * (1.0 - s))


def norm_back(grad, normed, inverse):
    return inverse * (
        grad
        - jnp.mean(grad, axis=0, keepdims=True)
        - normed * jnp.mean(grad * normed, axis=0, keepdims=True)
    )


def onehot(match):
    return match.astype(F32).astype(BF16)


def each(lower, upper, act):
    def step(k, carry):
        act(k)
        return carry

    lax.fori_loop(lower, upper, step, 0)


def remote(src, dst, send_sem, recv_sem, peer):
    return pltpu.make_async_remote_copy(
        src_ref=src,
        dst_ref=dst,
        send_sem=send_sem,
        recv_sem=recv_sem,
        device_id=peer,
        device_id_type=MESH,
    )


def wait_bytes(ref, sem):
    pltpu.make_async_copy(ref, ref, sem).wait()


def tile16(start):
    return pl.ds(pl.multiple_of(start, CAP), CAP)


def step_kernel(
    n_wide, n, table_ref, ids_ref, len_ref, w_hbm, wo_hbm, cot_hbm, out_ref, sum_ref,
    tab, tabb, w_ref, wo_ref, cot_ref, wt, asks, asked, picks, reply, replies, lanes, hot,
    emb, hid, normed1, qkv_out, qkv, keys, vals, wts, slopes, heads_out, heads, gm, gu,
    gatt_out, gatt, dq, dk, dv, back_out, back, gh, up_t, ge, outgoing, arriving, sib_out, sib_in,
    load_sem, ask_sem, reply_sem, lane_sem, nss, nrs, give_sem, sib_ss, sib_rs, col_ss, col_rs,
    pass_ss, pass_rs,
):
    wide = lax.axis_index("wide")
    me = lax.axis_index("narrow")
    chip = me // 2
    core = lax.rem(me, 2)
    chips = n // 2
    rows_dev, width = table_ref.shape
    tokens = ids_ref.shape[1]
    att = HEADS * HD
    slots = n_wide * CAP
    cols = width // chips

    def at_wide(k):
        return lax.rem(wide + k, n_wide)

    def at_chip(k):
        return lax.rem(chip + k, chips)

    barrier = pltpu.get_barrier_semaphore()

    def hail(peer):
        pl.semaphore_signal(barrier, inc=1, device_id=peer, device_id_type=MESH)

    each(
        1,
        n_wide * chips,
        lambda k: hail({"wide": at_wide(k // chips), "narrow": at_chip(lax.rem(k, chips)) * 2 + core}),
    )
    each(0, chips, lambda k: hail({"wide": wide, "narrow": at_chip(k) * 2 + 1 - core}))

    loads = [
        pltpu.make_async_copy(src, dst, load_sem.at[i])
        for i, (src, dst) in enumerate(
            ((table_ref, tab), (w_hbm, w_ref), (wo_hbm, wo_ref), (cot_hbm, cot_ref))
        )
    ]
    for load in loads:
        load.start()

    ids = ids_ref[...]
    owner = ids // rows_dev
    row = ids - owner * rows_dev
    hits_f = (owner == iota((n_wide, tokens), 0)).astype(F32)
    before = onehot(iota((tokens, tokens), 0) < iota((tokens, tokens), 1))
    earlier = mm(hits_f.astype(BF16), before)
    slot = jnp.sum(earlier * hits_f, axis=0, keepdims=True).astype(jnp.int32)
    target = owner * CAP + slot
    place = slot + CAP * lax.rem(wide, 8)
    at_place = onehot(place == iota((128, tokens), 0))
    high = row // 256
    low = row - high * 256
    high_m = (hits_f * high.astype(F32)).astype(BF16)
    low_m = (hits_f * low.astype(F32)).astype(BF16)
    wanted = (mm(high_m, at_place, NT) * 256.0 + mm(low_m, at_place, NT)).astype(jnp.int32)
    for o in range(n_wide):
        asks[o] = wanted[o : o + 1, :]

    pl.semaphore_wait(barrier, n_wide * chips - 1 + chips)

    def ask(k):
        peer = at_wide(k)
        remote(
            asks.at[peer], asked.at[wide], ask_sem.at[0], ask_sem.at[1], {"wide": peer}
        ).start()

    each(1, n_wide, ask)
    asked[wide] = asks[wide]
    loads[0].wait()
    tabb[...] = tab[...].astype(BF16)
    wait_bytes(asked.at[pl.ds(0, n_wide - 1)], ask_sem.at[1])

    lane16 = iota((CAP, 128), 1)
    sub16 = iota((CAP, 128), 0)
    row_iota = iota((CAP, rows_dev), 1)

    def answer(k):
        peer = at_wide(k)
        remote(
            reply.at[tile16(k * CAP)],
            replies.at[tile16(wide * CAP)],
            reply_sem.at[0],
            reply_sem.at[1],
            {"wide": peer},
        ).start()

    half = n_wide // 2
    for part in range(2):
        for k in range(part * half, (part + 1) * half):
            peer = at_wide(k)
            line = jnp.broadcast_to(asked[peer], (CAP, 128)).astype(F32)
            mine = lane16 == sub16 + CAP * lax.rem(peer, 8)
            column = jnp.sum(jnp.where(mine, line, 0.0), axis=1, keepdims=True).astype(jnp.int32)
            picks[CAP * k : CAP * (k + 1), :] = onehot(column == row_iota)
        lo = part * half * CAP
        reply[lo : lo + half * CAP, :] = mm(picks[lo : lo + half * CAP, :], tabb[...]).astype(BF16)
        each(max(1, part * half), (part + 1) * half, answer)
    replies[tile16(wide * CAP), :] = reply[:CAP, :]

    for g in range(n_wide // 8):
        total = asked[8 * g]
        for j in range(1, 8):
            total = total + asked[8 * g + j]
        lanes[chip, g : g + 1, :] = total
    for k in range(1, chips):
        remote(
            lanes.at[chip], lanes.at[chip], lane_sem.at[0], lane_sem.at[1],
            {"narrow": at_chip(k) * 2 + core},
        ).start()

    target_t = jnp.transpose(jnp.broadcast_to(target.astype(F32), (128, tokens))).astype(jnp.int32)
    take = jnp.concatenate(
        [onehot(target_t == iota((tokens, 128), 1) + 128 * g) for g in range(slots // 128)],
        axis=1,
    )

    length = len_ref[0]
    live = iota((tokens, 1), 0) + me * tokens < length
    live_t = iota((1, tokens), 1) + me * tokens < length
    for load in loads[1:]:
        load.wait()
    chunk = 256
    eye = onehot(iota((chunk, chunk), 0) == iota((chunk, chunk), 1))
    total_w = w_ref.shape[1]
    for c in range(total_w // chunk):
        part = slice(c * chunk, (c + 1) * chunk)
        wt[part, :] = mm(eye, w_ref[:, part], NT).astype(BF16)
    upstream = jnp.where(live, cot_ref[...], jnp.zeros((), BF16))
    gm[...] = mm(wo_ref[...], upstream, NT)
    up_t[...] = jnp.transpose(upstream.astype(F32))
    wait_bytes(lanes.at[pl.ds(0, chips - 1)], lane_sem.at[1])
    for y in range(chips):
        for g in range(slots // 128):
            lo = y * slots + 128 * g
            hot[:, lo : lo + 128] = onehot(iota((rows_dev, 128), 0) == lanes[y, g : g + 1, :])
    wait_bytes(replies.at[pl.ds(0, slots - CAP)], reply_sem.at[1])
    emb[...] = mm(take, replies[...])

    def exchange(step, source, landing, peer):
        return remote(
            source.at[peer],
            landing.at[me],
            nss.at[step, peer],
            nrs.at[step, me],
            {"narrow": peer},
        )

    def arrive(step, landing, peer):
        wait_bytes(landing.at[peer], nrs.at[step, peer])

    emb_t = jnp.transpose(emb[...])
    center = emb_t - jnp.mean(emb_t, axis=0, keepdims=True)
    inverse1 = lax.rsqrt(jnp.mean(center * center, axis=0, keepdims=True) + EPS)
    normed = center * inverse1
    normed1[...] = normed
    normed_b = normed.astype(BF16)
    for c in range(att // chunk, total_w // chunk):
        hid[c * chunk : (c + 1) * chunk, :] = mm(wt[c * chunk : (c + 1) * chunk, :], normed_b)

    def send_head(k):
        peer = lax.rem(me + k, n)
        base = pl.multiple_of(att + 3 * HD * peer, HD)
        qkv_out[peer, :HD, :] = hid[pl.ds(base, HD), :].astype(BF16)
        qkv_out[peer, HD:, :] = silu(hid[pl.ds(base + HD, 2 * HD), :]).astype(BF16)
        exchange(0, qkv_out, qkv, peer).start()

    each(1, n, send_head)
    base = pl.multiple_of(att + 3 * HD * me, HD)
    qkv[me, :HD, :] = hid[pl.ds(base, HD), :].astype(BF16)
    qkv[me, HD:, :] = silu(hid[pl.ds(base + HD, 2 * HD), :]).astype(BF16)

    for c in range(att // chunk):
        hid[c * chunk : (c + 1) * chunk, :] = mm(wt[c * chunk : (c + 1) * chunk, :], normed_b)
    each(1, n, lambda k: arrive(0, qkv, lax.rem(me + k, n)))

    scale = HD**-0.5
    for b in range(n):
        vals[b] = jnp.transpose(qkv[b, :HD, :].astype(F32)).astype(BF16)
        keys[b] = jnp.transpose(qkv[b, 2 * HD :, :].astype(F32)).astype(BF16)
    causal = iota((tokens, tokens), 0) <= iota((tokens, tokens), 1)
    for i in reversed(range(n)):
        query = qkv[i, HD : 2 * HD, :] * scale
        attended = jnp.zeros((HD, tokens), F32)
        for j in range(i + 1):
            scores = mm(keys[j], query)
            s = sigmoid(scores)
            weight = scores * s
            slope = s + weight * (1.0 - s)
            if i == j:
                weight = jnp.where(causal, weight, 0.0)
                slope = jnp.where(causal, slope, 0.0)
            weight = weight.astype(BF16)
            wts[j, i] = weight
            slopes[j, i] = slope.astype(BF16)
            attended = attended + mm(qkv[j, :HD, :], weight)
        heads_out[i] = attended.astype(BF16)

        @pl.when(i != me)
        def _():
            exchange(1, heads_out, heads, i).start()

        @pl.when(i == me)
        def _():
            heads[i] = heads_out[i]

    each(1, n, lambda k: arrive(1, heads, lax.rem(me + k, n)))

    merged = heads[...].astype(F32).reshape(att, tokens)
    center = merged - jnp.mean(merged, axis=0, keepdims=True)
    inverse2 = lax.rsqrt(jnp.mean(center * center, axis=0, keepdims=True) + EPS)
    normed2 = center * inverse2
    gate = silu(hid[:att, :]).astype(BF16).astype(F32)
    grad_mixed = gm[...]
    gu[...] = grad_mixed * normed2
    grad_att = norm_back(grad_mixed * gate, normed2, inverse2).astype(BF16)
    gatt_out[...] = grad_att.reshape(n, HD, tokens)
    each(1, n, lambda k: exchange(2, gatt_out, gatt, lax.rem(me + k, n)).start())
    gatt[me] = gatt_out[me]
    mixed = jnp.transpose(normed2 * gate).astype(BF16)
    result = emb[...] + mm(mixed, wo_ref[...])
    out_ref[...] = jnp.where(live, result, 0.0).astype(BF16)
    gh[:att, :] = (gu[...] * silu_slope(hid[:att, :])).astype(BF16)
    dk[...] = jnp.zeros_like(dk)
    dv[...] = jnp.zeros_like(dv)

    for i in reversed(range(n)):

        @pl.when(i != me)
        def _():
            arrive(2, gatt, i)

        grad = gatt[i]
        query = qkv[i, HD : 2 * HD, :]
        dq = jnp.zeros((HD, tokens), F32)
        for j in range(i + 1):
            dw = mm(vals[j], grad)
            ds = (dw * slopes[j, i].astype(F32)).astype(BF16)
            dv[j] += mm(grad, wts[j, i], NT)
            dk[j] += mm(query, ds, NT)
            dq = dq + mm(qkv[j, 2 * HD :, :], ds)
        back_out[i, :HD, :] = dv[i].astype(BF16)
        back_out[i, HD : 2 * HD, :] = (dq * scale).astype(BF16)
        back_out[i, 2 * HD :, :] = (dk[i] * scale).astype(BF16)

        @pl.when(i != me)
        def _():
            exchange(3, back_out, back, i).start()

        @pl.when(i == me)
        def _():
            back[i] = back_out[i]

    hid[att:, :] = silu_slope(hid[att:, :])
    put = onehot(iota((slots, tokens), 0) == target)
    each(1, n, lambda k: arrive(3, back, lax.rem(me + k, n)))
    for h in range(HEADS):
        base = att + 3 * HD * h
        gh[base : base + HD, :] = back[h, :HD, :]
        gh[base + HD : base + 3 * HD, :] = (
            back[h, HD:, :].astype(F32) * hid[base + HD : base + 3 * HD, :]
        ).astype(BF16)
    grad_norm1 = mm(w_ref[...], gh[...])
    grad_emb = norm_back(grad_norm1, normed1[...], inverse1) + up_t[...]
    ge[...] = jnp.where(live_t, grad_emb, 0.0).astype(BF16)

    own = tile16(chip * slots + wide * CAP)

    def give(k, y):
        o = at_wide(k)
        remote(
            outgoing.at[tile16(y * slots + o * CAP)],
            arriving.at[own],
            give_sem.at[0],
            give_sem.at[1],
            {"wide": o, "narrow": y * 2 + core},
        ).start()

    for q in range(chips):
        y = at_chip(q)
        block = ge[pl.ds(pl.multiple_of(y * cols, cols), cols), :]
        outgoing[pl.ds(pl.multiple_of(y * slots, slots), slots), :] = mm(put, block, NT).astype(BF16)
        each(1 if q == 0 else 0, n_wide, lambda k: give(k, y))
    arriving[own, :] = outgoing[own, :]
    wait_bytes(arriving.at[pl.ds(0, chips * slots - CAP)], give_sem.at[1])

    half_rows = rows_dev // 2
    parts = 4
    piece = half_rows // parts
    sibling = {"narrow": chip * 2 + 1 - core}

    def rows_at(side, p):
        return pl.ds(pl.multiple_of(side * half_rows + p * piece, piece), piece)

    def swap(p):
        return remote(sib_out.at[p], sib_in.at[p], sib_ss.at[p], sib_rs.at[p], sibling)

    def collect(k, p):
        spot = sum_ref.at[chip, rows_at(core, p)]
        return remote(
            spot, spot, col_ss.at[k, p], col_rs.at[k, p], {"narrow": at_chip(k) * 2 + core}
        )

    def pass_on(k, p):
        spot = sum_ref.at[at_chip(chips - k), rows_at(core, p)]
        return remote(spot, spot, pass_ss.at[k, p], pass_rs.at[k, p], sibling)

    for p in range(parts):
        sib_out[p] = mm(hot[rows_at(1 - core, p), :], arriving[...]).astype(BF16)
        swap(p).start()
    for p in range(parts):
        total = mm(hot[rows_at(core, p), :], arriving[...])
        swap(p).wait_recv()
        sum_ref[chip, rows_at(core, p), :] = (total + sib_in[p].astype(F32)).astype(BF16)
        for k in range(1, chips):
            collect(k, p).start()
        pass_on(0, p).start()
    for p in range(parts):
        for k in range(1, chips):
            collect(k, p).wait_recv()
            pass_on(k, p).start()
    for p in range(parts):
        for k in range(chips):
            pass_on(k, p).wait_recv()

    wait_bytes(asks.at[pl.ds(0, n_wide - 1)], ask_sem.at[0])
    wait_bytes(reply.at[pl.ds(0, slots - CAP)], reply_sem.at[0])
    wait_bytes(lanes.at[pl.ds(0, chips - 1)], lane_sem.at[0])
    wait_bytes(outgoing.at[pl.ds(0, chips * slots - CAP)], give_sem.at[0])

    def sent(k):
        peer = lax.rem(me + k, n)
        for step, source in enumerate((qkv_out, heads_out, gatt_out, back_out)):
            wait_bytes(source.at[peer], nss.at[step, peer])

    each(1, n, sent)
    for p in range(parts):
        swap(p).wait_send()
        for k in range(1, chips):
            collect(k, p).wait_send()
        for k in range(chips):
            pass_on(k, p).wait_send()


def run_step(n_wide, n, table, ids, lengths, w_uvqk, w_out, cotangent):
    rows_dev, width = table.shape
    tokens = ids.shape[1]
    att = HEADS * HD
    chips = n // 2
    slots = n_wide * CAP
    cols = width // chips
    parts = 4
    vmem = pl.BlockSpec(memory_space=pltpu.VMEM)
    hbm = pl.BlockSpec(memory_space=pl.ANY)
    dma = pltpu.SemaphoreType.DMA
    return pl.pallas_call(
        functools.partial(step_kernel, n_wide, n),
        out_shape=(
            jax.ShapeDtypeStruct((tokens, width), BF16),
            jax.ShapeDtypeStruct((chips, rows_dev, cols), BF16),
        ),
        in_specs=[hbm, vmem, pl.BlockSpec(memory_space=pltpu.SMEM), hbm, hbm, hbm],
        out_specs=(vmem, vmem),
        scratch_shapes=[
            pltpu.VMEM((rows_dev, width), F32),
            pltpu.VMEM((rows_dev, width), BF16),
            pltpu.VMEM(w_uvqk.shape, BF16),
            pltpu.VMEM(w_out.shape, BF16),
            pltpu.VMEM((tokens, width), BF16),
            pltpu.VMEM((w_uvqk.shape[1], width), BF16),
            pltpu.VMEM((n_wide, 1, 128), jnp.int32),
            pltpu.VMEM((n_wide, 1, 128), jnp.int32),
            pltpu.VMEM((slots, rows_dev), BF16),
            pltpu.VMEM((slots, width), BF16),
            pltpu.VMEM((slots, width), BF16),
            pltpu.VMEM((chips, n_wide // 8, 128), jnp.int32),
            pltpu.VMEM((rows_dev, chips * slots), BF16),
            pltpu.VMEM((tokens, width), F32),
            pltpu.VMEM((4 * att, tokens), F32),
            pltpu.VMEM((width, tokens), F32),
            pltpu.VMEM((n, 3 * HD, tokens), BF16),
            pltpu.VMEM((n, 3 * HD, tokens), BF16),
            pltpu.VMEM((n, tokens, HD), BF16),
            pltpu.VMEM((n, tokens, HD), BF16),
            pltpu.VMEM((n, n, tokens, tokens), BF16),
            pltpu.VMEM((n, n, tokens, tokens), BF16),
            pltpu.VMEM((n, HD, tokens), BF16),
            pltpu.VMEM((n, HD, tokens), BF16),
            pltpu.VMEM((att, tokens), F32),
            pltpu.VMEM((att, tokens), F32),
            pltpu.VMEM((n, HD, tokens), BF16),
            pltpu.VMEM((n, HD, tokens), BF16),
            pltpu.VMEM((8, 128), F32),
            pltpu.VMEM((n, HD, tokens), F32),
            pltpu.VMEM((n, HD, tokens), F32),
            pltpu.VMEM((n, 3 * HD, tokens), BF16),
            pltpu.VMEM((n, 3 * HD, tokens), BF16),
            pltpu.VMEM((4 * att, tokens), BF16),
            pltpu.VMEM((width, tokens), F32),
            pltpu.VMEM((width, tokens), BF16),
            pltpu.VMEM((chips * slots, cols), BF16),
            pltpu.VMEM((chips * slots, cols), BF16),
            pltpu.VMEM((parts, rows_dev // 2 // parts, cols), BF16),
            pltpu.VMEM((parts, rows_dev // 2 // parts, cols), BF16),
            dma((4,)),
            dma((2,)),
            dma((2,)),
            dma((2,)),
            dma((4, n)),
            dma((4, n)),
            dma((2,)),
            dma((parts,)),
            dma((parts,)),
            dma((chips, parts)),
            dma((chips, parts)),
            dma((chips, parts)),
            dma((chips, parts)),
        ],
        compiler_params=pltpu.CompilerParams(
            collective_id=0, has_side_effects=True, vmem_limit_bytes=60 * MIB
        ),
    )(table, ids, lengths, w_uvqk, w_out, cotangent)


def update_kernel(sum_ref, table_ref, accum_ref, out_in, new_table_ref, new_accum_ref, out_out, sem):
    step = pl.program_id(0)
    copy = pltpu.make_async_copy(out_in, out_out, sem)

    @pl.when(step == 0)
    def _():
        copy.start()

    chips, rows, cols = sum_ref.shape
    width = chips * cols
    groups = rows // 128
    for g in range(groups):
        part = slice(g * 128, (g + 1) * 128)
        grads = [sum_ref[y, part, :].astype(F32) for y in range(chips)]
        square = sum(v * v for v in grads)
        mean = jnp.sum(square, axis=1, keepdims=True) * (1.0 / width)
        line = jnp.transpose(jnp.broadcast_to(mean, (128, 128)))[:1, :]
        spot = pl.ds(step * groups + g, 1)
        accum = accum_ref[spot, :] + line
        new_accum_ref[spot, :] = accum
        factor = jnp.transpose(jnp.broadcast_to(RATE * lax.rsqrt(accum), (128, 128)))
        for y in range(chips):
            lane = slice(y * cols, (y + 1) * cols)
            new_table_ref[part, lane] = table_ref[part, lane] - grads[y] * factor

    @pl.when(step == pl.num_programs(0) - 1)
    def _():
        copy.wait()


def update(summed, table, accum, output):
    rows_dev, width = table.shape
    chips, _, cols = summed.shape
    block = min(512, rows_dev)
    whole = pl.BlockSpec((rows_dev // 128, 128), lambda i: (0, 0))
    rows = pl.BlockSpec((block, width), lambda i: (i, 0))
    hbm = pl.BlockSpec(memory_space=pl.ANY)
    new_table, new_accum, result = pl.pallas_call(
        update_kernel,
        grid=(rows_dev // block,),
        out_shape=(
            jax.ShapeDtypeStruct(table.shape, F32),
            jax.ShapeDtypeStruct((rows_dev // 128, 128), F32),
            jax.ShapeDtypeStruct(output.shape, output.dtype),
        ),
        in_specs=[pl.BlockSpec((chips, block, cols), lambda i: (0, i, 0)), rows, whole, hbm],
        out_specs=(rows, whole, hbm),
        scratch_shapes=[pltpu.SemaphoreType.DMA],
        compiler_params=pltpu.CompilerParams(vmem_limit_bytes=24 * MIB),
    )(summed, table, accum.reshape(rows_dev // 128, 128), output)
    return new_table, new_accum.reshape(rows_dev), result


def local(table, accum, ids, lengths, w_uvqk, w_out, cotangent):
    n_wide = lax.axis_size("wide")
    n_narrow = lax.axis_size("narrow")
    width = table.shape[1]
    tokens = ids.shape[1]
    output, summed = run_step(
        n_wide, n_narrow, table, ids, lengths, w_uvqk, w_out, cotangent.reshape(tokens, width)
    )
    new_table, new_accum, output = update(summed, table, accum, output)
    return (output.reshape(1, tokens, width), new_table, new_accum)


def solution(mesh):
    in_specs = (
        P("wide", None),
        P("wide"),
        P("wide", "narrow"),
        P("wide"),
        P(),
        P(),
        P("wide", "narrow", None),
    )
    out_specs = (P("wide", "narrow", None), P("wide", None), P("wide"))
    return jax.shard_map(local, mesh=mesh, in_specs=in_specs, out_specs=out_specs, check_vma=False)
```

```python
import functools

import jax
import jax.numpy as jnp
from jax import lax
from jax.experimental import pallas as pl
from jax.experimental.pallas import tpu as pltpu
from jax.sharding import PartitionSpec as P

HEADS = 8
HD = 64
CAP = 16
EPS = 1e-05
RATE = 0.5
MESH = pl.DeviceIdType.MESH
F32 = jnp.float32
BF16 = jnp.bfloat16
MIB = 1 << 20
Z = 8
X = 4
DZ = (4, 3, 5, 2, 6, 1, 7, 0)
DX = (2, 1, 3, 0)
DY = (2, 1, 3, 0)
AROUND = [(dz, dx) for dx in DX for dz in DZ]

NN = (((1,), (0,)), ((), ()))
NT = (((1,), (1,)), ((), ()))
TN = (((0,), (0,)), ((), ()))


def mm(a, b, dims=NN):
    return lax.dot_general(a, b, dims, preferred_element_type=F32)


def iota(shape, dim):
    return lax.broadcasted_iota(jnp.int32, shape, dim)


def sigmoid(t):
    return 0.5 * jnp.tanh(0.5 * t) + 0.5


def silu(t):
    return t * sigmoid(t)


def silu_slope(t):
    s = sigmoid(t)
    return s * (1.0 + t * (1.0 - s))


def norm_back(grad, normed, inverse):
    return inverse * (
        grad
        - jnp.mean(grad, axis=0, keepdims=True)
        - normed * jnp.mean(grad * normed, axis=0, keepdims=True)
    )


def onehot(match):
    return match.astype(F32).astype(BF16)


def each(lower, upper, act):
    def step(k, carry):
        act(k)
        return carry

    lax.fori_loop(lower, upper, step, 0)


def remote(src, dst, send_sem, recv_sem, peer):
    return pltpu.make_async_remote_copy(
        src_ref=src,
        dst_ref=dst,
        send_sem=send_sem,
        recv_sem=recv_sem,
        device_id=peer,
        device_id_type=MESH,
    )


def wait_bytes(ref, sem):
    pltpu.make_async_copy(ref, ref, sem).wait()


def tile16(start):
    return pl.ds(pl.multiple_of(start, CAP), CAP)


def step_kernel(
    n_wide, n, table_ref, accum_ref, ids_ref, len_ref, w_hbm, wo_hbm, cot_hbm,
    out_ref, new_table_ref, new_accum_ref, sum_ref,
    tab, w_ref, wo_ref, cot_ref, wt, asks, asked, reply, replies, lanes, hot,
    emb, hid, normed1, qk_out, qk, v_out, v_in, keys, vals, wts, slopes, heads_out, heads, gm, gu,
    gatt_out, gatt, dk, dv, back_out, back, gh, up_t, ge, outgoing, arriving, sib_out, sib_in,
    load_sem, ask_sem, reply_sem, lane_sem, nss, nrs, give_sem, sib_ss, sib_rs, ring_ss, ring_rs,
    pass_ss, pass_rs,
):
    wide = lax.axis_index("wide")
    me = lax.axis_index("narrow")
    chip = me // 2
    core = lax.rem(me, 2)
    chips = n // 2
    rows_dev, width = table_ref.shape
    tokens = ids_ref.shape[1]
    att = HEADS * HD
    slots = n_wide * CAP
    cols = width // chips

    depth, across = wide // X, lax.rem(wide, X)
    zs = [lax.rem(depth + d, Z) * X for d in range(Z)]
    xs = [lax.rem(across + d, X) for d in range(X)]
    ys = [lax.rem(chip + d, chips) for d in range(chips)]

    def far(dz, dx):
        return zs[dz] + xs[dx]

    finish = []
    barrier = pltpu.get_barrier_semaphore()

    def hail(peer):
        pl.semaphore_signal(barrier, inc=1, device_id=peer, device_id_type=MESH)

    for dz, dx in AROUND:
        for dy in DY:
            if dz or dx or dy:
                hail({"wide": far(dz, dx), "narrow": ys[dy] * 2 + core})
    for dy in DY:
        hail({"wide": wide, "narrow": ys[dy] * 2 + 1 - core})

    loads = [
        pltpu.make_async_copy(src, dst, load_sem.at[i])
        for i, (src, dst) in enumerate(
            ((table_ref, tab), (w_hbm, w_ref), (wo_hbm, wo_ref), (cot_hbm, cot_ref))
        )
    ]
    for load in loads:
        load.start()

    ids = ids_ref[...]
    bits = rows_dev.bit_length() - 1
    owner = lax.shift_right_logical(ids, bits)
    row = ids - owner * rows_dev
    hits_f = (owner == iota((n_wide, tokens), 0)).astype(F32)
    before = onehot(iota((tokens, tokens), 0) < iota((tokens, tokens), 1))
    earlier = mm(hits_f.astype(BF16), before)
    slot = jnp.sum(earlier * hits_f, axis=0, keepdims=True).astype(jnp.int32)
    target = owner * CAP + slot
    place = slot + CAP * lax.rem(wide, 8)
    at_place = onehot(place == iota((128, tokens), 0))
    high = lax.shift_right_logical(row, 8)
    low = row - high * 256
    high_m = (hits_f * high.astype(F32)).astype(BF16)
    low_m = (hits_f * low.astype(F32)).astype(BF16)
    wanted = (mm(high_m, at_place, NT) * 256.0 + mm(low_m, at_place, NT)).astype(jnp.int32)
    for o in range(n_wide):
        asks[o] = wanted[o : o + 1, :]

    pl.semaphore_wait(barrier, n_wide * chips - 1 + chips)

    for dz, dx in AROUND[:-1]:
        peer = far(dz, dx)
        remote(
            asks.at[peer], asked.at[wide], ask_sem.at[0], ask_sem.at[1], {"wide": peer}
        ).start()
    finish.append(lambda: wait_bytes(asks.at[pl.ds(0, n_wide - 1)], ask_sem.at[0]))
    asked[wide] = asks[wide]
    loads[0].wait()
    wt[...] = tab[...].astype(BF16)
    wait_bytes(asked.at[pl.ds(0, n_wide - 1)], ask_sem.at[1])

    lane16 = iota((CAP, 128), 1)
    sub16 = iota((CAP, 128), 0)
    row_iota = iota((CAP, rows_dev), 1)

    half = n_wide // 2
    for part in range(2):
        for k in range(part * half, (part + 1) * half):
            peer = far(*AROUND[k])
            line = jnp.broadcast_to(asked[peer], (CAP, 128)).astype(F32)
            mine = lane16 == sub16 + CAP * lax.rem(peer, 8)
            column = jnp.sum(jnp.where(mine, line, 0.0), axis=1, keepdims=True).astype(jnp.int32)
            hot[CAP * k : CAP * (k + 1), :] = onehot(column == row_iota)
        lo = part * half * CAP
        reply[lo : lo + half * CAP, :] = mm(hot[lo : lo + half * CAP, :], wt[...]).astype(BF16)
        for k in range(part * half, min((part + 1) * half, n_wide - 1)):
            remote(
                reply.at[pl.ds(k * CAP, CAP)],
                replies.at[tile16(wide * CAP)],
                reply_sem.at[0],
                reply_sem.at[1],
                {"wide": far(*AROUND[k])},
            ).start()
    replies[tile16(wide * CAP), :] = reply[slots - CAP :, :]
    finish.append(lambda: wait_bytes(reply.at[pl.ds(0, slots - CAP)], reply_sem.at[0]))

    for g in range(n_wide // 8):
        total = asked[8 * g]
        for j in range(1, 8):
            total = total + asked[8 * g + j]
        lanes[chip, g : g + 1, :] = total
    for k in range(1, chips):
        remote(
            lanes.at[chip], lanes.at[chip], lane_sem.at[0], lane_sem.at[1],
            {"narrow": ys[k] * 2 + core},
        ).start()
    finish.append(lambda: wait_bytes(lanes.at[pl.ds(0, chips - 1)], lane_sem.at[0]))

    target_t = jnp.transpose(jnp.broadcast_to(target.astype(F32), (128, tokens))).astype(jnp.int32)
    take = jnp.concatenate(
        [onehot(target_t == iota((tokens, 128), 1) + 128 * g) for g in range(slots // 128)],
        axis=1,
    )

    length = len_ref[0]
    live = iota((tokens, 1), 0) + me * tokens < length
    live_t = iota((1, tokens), 1) + me * tokens < length
    for load in loads[1:]:
        load.wait()
    chunk = 256
    eye = onehot(iota((chunk, chunk), 0) == iota((chunk, chunk), 1))
    total_w = w_ref.shape[1]
    for c in range(total_w // chunk):
        part = slice(c * chunk, (c + 1) * chunk)
        wt[part, :] = mm(eye, w_ref[:, part], NT).astype(BF16)
    upstream = jnp.where(live, cot_ref[...], jnp.zeros((), BF16))
    gm[...] = mm(wo_ref[...], upstream, NT)
    up_t[...] = jnp.transpose(upstream.astype(F32))
    wait_bytes(lanes.at[pl.ds(0, chips - 1)], lane_sem.at[1])
    for y in range(chips):
        for g in range(slots // 128):
            lo = y * slots + 128 * g
            hot[:, lo : lo + 128] = onehot(iota((rows_dev, 128), 0) == lanes[y, g : g + 1, :])
    wait_bytes(replies.at[pl.ds(0, slots - CAP)], reply_sem.at[1])
    emb[...] = mm(take, replies[...])

    def exchange(step, source, landing, peer):
        return remote(
            source.at[peer],
            landing.at[me],
            nss.at[step, peer],
            nrs.at[step, me],
            {"narrow": peer},
        )

    def arrive(step, landing, peer):
        wait_bytes(landing.at[peer], nrs.at[step, peer])

    def sent(step, source):
        def one(k):
            peer = lax.rem(me + k, n)
            wait_bytes(source.at[peer], nss.at[step, peer])

        return lambda: each(1, n, one)

    emb_t = jnp.transpose(emb[...])
    center = emb_t - jnp.mean(emb_t, axis=0, keepdims=True)
    inverse1 = lax.rsqrt(jnp.mean(center * center, axis=0, keepdims=True) + EPS)
    normed = center * inverse1
    normed1[...] = normed
    normed_b = normed.astype(BF16)
    for c in range(att // chunk, total_w // chunk):
        hid[c * chunk : (c + 1) * chunk, :] = mm(wt[c * chunk : (c + 1) * chunk, :], normed_b)

    def send_head(k):
        peer = lax.rem(me + k, n)
        base = pl.multiple_of(att + 3 * HD * peer, HD)
        qk_out[peer] = silu(hid[pl.ds(base + HD, 2 * HD), :]).astype(BF16)
        exchange(0, qk_out, qk, peer).start()

    def send_values(k):
        peer = lax.rem(me + k, n)
        base = pl.multiple_of(att + 3 * HD * peer, HD)
        v_out[peer] = hid[pl.ds(base, HD), :].astype(BF16)
        exchange(4, v_out, v_in, peer).start()

    each(1, n, send_head)
    each(1, n, send_values)
    finish.append(sent(0, qk_out))
    finish.append(sent(4, v_out))
    base = pl.multiple_of(att + 3 * HD * me, HD)
    qk[me] = silu(hid[pl.ds(base + HD, 2 * HD), :]).astype(BF16)
    v_in[me] = hid[pl.ds(base, HD), :].astype(BF16)

    for c in range(att // chunk):
        hid[c * chunk : (c + 1) * chunk, :] = mm(wt[c * chunk : (c + 1) * chunk, :], normed_b)
    each(1, n, lambda k: arrive(0, qk, lax.rem(me + k, n)))

    scale = HD**-0.5
    for b in range(n):
        keys[b] = jnp.transpose(qk[b, HD:, :].astype(F32)).astype(BF16)
    causal = iota((tokens, tokens), 0) <= iota((tokens, tokens), 1)

    def tri(j, i):
        return i * (i + 1) // 2 + j

    def weigh(j, i, query):
        score = mm(keys[j], query)
        twice = 1.0 + jnp.tanh(score)
        weight = score * twice
        slope = twice + weight * (2.0 - twice)
        if i == j:
            weight = jnp.where(causal, weight, 0.0)
            slope = jnp.where(causal, slope, 0.0)
        weight = weight.astype(BF16)
        wts[tri(j, i)] = weight
        slopes[tri(j, i)] = slope.astype(BF16)
        return weight

    def send_block(step, source, landing, i):
        @pl.when(i != me)
        def _():
            exchange(step, source, landing, i).start()

        @pl.when(i == me)
        def _():
            landing[i] = source[i]

    early = 2
    for i in range(n - 1, n - 1 - early, -1):
        query = qk[i, :HD, :] * (0.5 * scale)
        for j in range(i + 1):
            weigh(j, i, query)
    each(1, n, lambda k: arrive(4, v_in, lax.rem(me + k, n)))
    for i in reversed(range(n)):
        query = qk[i, :HD, :] * (0.5 * scale)
        attended = jnp.zeros((HD, tokens), F32)
        for j in range(i + 1):
            weight = weigh(j, i, query) if i < n - early else wts[tri(j, i)]
            attended = attended + mm(v_in[j], weight)
        heads_out[i] = attended.astype(BF16)
        send_block(1, heads_out, heads, i)
    for b in range(n):
        vals[b] = jnp.transpose(v_in[b].astype(F32)).astype(BF16)

    finish.append(sent(1, heads_out))
    each(1, n, lambda k: arrive(1, heads, lax.rem(me + k, n)))

    merged = heads[...].astype(F32).reshape(att, tokens)
    center = merged - jnp.mean(merged, axis=0, keepdims=True)
    inverse2 = lax.rsqrt(jnp.mean(center * center, axis=0, keepdims=True) + EPS)
    normed2 = center * inverse2
    gate = silu(hid[:att, :]).astype(BF16).astype(F32)
    grad_mixed = gm[...]
    gu[...] = grad_mixed * normed2
    grad_att = norm_back(grad_mixed * gate, normed2, inverse2).astype(BF16)
    gatt_out[...] = grad_att.reshape(n, HD, tokens)
    each(1, n, lambda k: exchange(2, gatt_out, gatt, lax.rem(me + k, n)).start())
    finish.append(sent(2, gatt_out))
    gatt[me] = gatt_out[me]
    mixed = jnp.transpose(normed2 * gate).astype(BF16)
    result = emb[...] + mm(mixed, wo_ref[...])
    out_ref[...] = jnp.where(live, result, 0.0).astype(BF16)
    gh[:att, :] = (gu[...] * silu_slope(hid[:att, :])).astype(BF16)
    dk[...] = jnp.zeros_like(dk)
    dv[...] = jnp.zeros_like(dv)

    for i in reversed(range(n)):

        @pl.when(i != me)
        def _():
            arrive(2, gatt, i)

        grad = gatt[i]
        query = qk[i, :HD, :]
        dq = jnp.zeros((HD, tokens), F32)
        for j in range(i + 1):
            dw = mm(vals[j], grad)
            ds = (dw * slopes[tri(j, i)].astype(F32)).astype(BF16)
            dv[j] += mm(grad, wts[tri(j, i)], NT)
            dk[j] += mm(query, ds, NT)
            dq = dq + mm(qk[j, HD:, :], ds)
        back_out[i, :HD, :] = dv[i].astype(BF16)
        back_out[i, HD : 2 * HD, :] = (dq * (0.5 * scale)).astype(BF16)
        back_out[i, 2 * HD :, :] = (dk[i] * (0.5 * scale)).astype(BF16)
        send_block(3, back_out, back, i)

    finish.append(sent(3, back_out))
    hid[att:, :] = silu_slope(hid[att:, :])
    put = onehot(iota((slots, tokens), 0) == target)
    each(1, n, lambda k: arrive(3, back, lax.rem(me + k, n)))
    for h in range(HEADS):
        base = att + 3 * HD * h
        gh[base : base + HD, :] = back[h, :HD, :]
        gh[base + HD : base + 3 * HD, :] = (
            back[h, HD:, :].astype(F32) * hid[base + HD : base + 3 * HD, :]
        ).astype(BF16)
    grad_norm1 = mm(w_ref[...], gh[...])
    grad_emb = norm_back(grad_norm1, normed1[...], inverse1) + up_t[...]
    ge[...] = jnp.where(live_t, grad_emb, 0.0).astype(BF16)

    own = tile16(chip * slots + wide * CAP)

    for dy in DY:
        y = ys[dy]
        block = ge[pl.ds(pl.multiple_of(y * cols, cols), cols), :]
        outgoing[pl.ds(pl.multiple_of(y * slots, slots), slots), :] = mm(put, block, NT).astype(BF16)
        for dz, dx in AROUND:
            if dz or dx or dy:
                o = far(dz, dx)
                remote(
                    outgoing.at[tile16(y * slots + o * CAP)],
                    arriving.at[own],
                    give_sem.at[0],
                    give_sem.at[1],
                    {"wide": o, "narrow": y * 2 + core},
                ).start()
    finish.append(lambda: wait_bytes(outgoing.at[pl.ds(0, chips * slots - CAP)], give_sem.at[0]))
    arriving[own, :] = outgoing[own, :]
    wait_bytes(arriving.at[pl.ds(0, chips * slots - CAP)], give_sem.at[1])

    half_rows = rows_dev // 2
    parts = 4
    piece = half_rows // parts
    sibling = {"narrow": chip * 2 + 1 - core}

    def rows_at(side, p):
        return pl.ds(pl.multiple_of(side * half_rows + p * piece, piece), piece)

    def swap(p):
        return remote(sib_out.at[p], sib_in.at[p], sib_ss.at[p], sib_rs.at[p], sibling)

    def ring(way, hop, p):
        spot = sum_ref.at[ys[(1 - hop) * way % chips], rows_at(core, p)]
        lane = 2 * hop - 2 + (way < 0)
        return remote(
            spot, spot, ring_ss.at[lane, p], ring_rs.at[lane, p], {"narrow": ys[way % chips] * 2 + core}
        )

    def pass_on(k, p):
        spot = sum_ref.at[ys[k], rows_at(core, p)]
        return remote(spot, spot, pass_ss.at[k, p], pass_rs.at[k, p], sibling)

    groups = piece // 128

    def update(side, p):
        first = side * (half_rows // 128) + p * groups
        for g in range(groups):
            part = pl.ds(pl.multiple_of(side * half_rows + p * piece + g * 128, 128), 128)
            grads = [sum_ref[y, part, :].astype(F32) for y in range(chips)]
            square = sum(v * v for v in grads)
            mean = jnp.sum(square, axis=1, keepdims=True) * (1.0 / width)
            line = jnp.transpose(jnp.broadcast_to(mean, (128, 128)))[:1, :]
            spot = pl.ds(first + g, 1)
            accum = accum_ref[spot, :] + line
            new_accum_ref[spot, :] = accum
            factor = jnp.transpose(jnp.broadcast_to(RATE * lax.rsqrt(accum), (128, 128)))
            for y in range(chips):
                lane = slice(y * cols, (y + 1) * cols)
                new_table_ref[part, lane] = tab[part, lane] - grads[y] * factor

    low, high = tuple(range(parts // 2)), tuple(range(parts // 2, parts))
    order = [p for pair in zip(low, high) for p in pair]
    for p in order:
        sib_out[p] = mm(hot[rows_at(1 - core, p), :], arriving[...]).astype(BF16)
        swap(p).start()
    for p in order:
        total = mm(hot[rows_at(core, p), :], arriving[...])
        swap(p).wait_recv()
        sum_ref[chip, rows_at(core, p), :] = (total + sib_in[p].astype(F32)).astype(BF16)
        ring(1 if p in low else -1, 1, p).start()
        pass_on(0, p).start()
    for p in order:
        ring(-1 if p in low else 1, 1, p).start()
    for p in order:
        way = 1 if p in low else -1
        ring(way, 1, p).wait_recv()
        ring(way, 2, p).start()
        pass_on(-way % chips, p).start()
    for at, p in enumerate(order):
        way = 1 if p in low else -1
        ring(-way, 1, p).wait_recv()
        pass_on(way % chips, p).start()
    for at, p in enumerate(order):
        way = 1 if p in low else -1
        ring(way, 2, p).wait_recv()
        pass_on(2, p).start()
        update(core, p)
        if at:
            q = order[at - 1]
            for k in range(chips):
                pass_on(k, q).wait_recv()
            update(1 - core, q)
    for k in range(chips):
        pass_on(k, order[-1]).wait_recv()
    update(1 - core, order[-1])

    for wait in finish:
        wait()
    for p in range(parts):
        swap(p).wait_send()
        for way in (1, -1):
            ring(way, 1, p).wait_send()
        ring(1 if p in low else -1, 2, p).wait_send()
        for k in range(chips):
            pass_on(k, p).wait_send()


def run_step(n_wide, n, table, accum, ids, lengths, w_uvqk, w_out, cotangent):
    rows_dev, width = table.shape
    tokens = ids.shape[1]
    att = HEADS * HD
    chips = n // 2
    slots = n_wide * CAP
    cols = width // chips
    parts = 4
    vmem = pl.BlockSpec(memory_space=pltpu.VMEM)
    hbm = pl.BlockSpec(memory_space=pltpu.HBM)
    dma = pltpu.SemaphoreType.DMA
    return pl.pallas_call(
        functools.partial(step_kernel, n_wide, n),
        out_shape=(
            pltpu.VMEM((tokens, width), BF16),
            pltpu.VMEM((rows_dev, width), F32),
            pltpu.VMEM((rows_dev // 128, 128), F32),
        ),
        in_specs=[hbm, vmem, vmem, pl.BlockSpec(memory_space=pltpu.SMEM), hbm, hbm, hbm],
        out_specs=(vmem, vmem, vmem),
        scratch_shapes=[
            pltpu.VMEM((chips, rows_dev, cols), BF16),
            pltpu.VMEM((rows_dev, width), F32),
            pltpu.VMEM(w_uvqk.shape, BF16),
            pltpu.VMEM(w_out.shape, BF16),
            pltpu.VMEM((tokens, width), BF16),
            pltpu.VMEM((w_uvqk.shape[1], width), BF16),
            pltpu.VMEM((n_wide, 1, 128), jnp.int32),
            pltpu.VMEM((n_wide, 1, 128), jnp.int32),
            pltpu.VMEM((slots, width), BF16),
            pltpu.VMEM((slots, width), BF16),
            pltpu.VMEM((chips, n_wide // 8, 128), jnp.int32),
            pltpu.VMEM((rows_dev, chips * slots), BF16),
            pltpu.VMEM((tokens, width), F32),
            pltpu.VMEM((4 * att, tokens), F32),
            pltpu.VMEM((width, tokens), F32),
            pltpu.VMEM((n, 2 * HD, tokens), BF16),
            pltpu.VMEM((n, 2 * HD, tokens), BF16),
            pltpu.VMEM((n, HD, tokens), BF16),
            pltpu.VMEM((n, HD, tokens), BF16),
            pltpu.VMEM((n, tokens, HD), BF16),
            pltpu.VMEM((n, tokens, HD), BF16),
            pltpu.VMEM((n * (n + 1) // 2, tokens, tokens), BF16),
            pltpu.VMEM((n * (n + 1) // 2, tokens, tokens), BF16),
            pltpu.VMEM((n, HD, tokens), BF16),
            pltpu.VMEM((n, HD, tokens), BF16),
            pltpu.VMEM((att, tokens), F32),
            pltpu.VMEM((att, tokens), F32),
            pltpu.VMEM((n, HD, tokens), BF16),
            pltpu.VMEM((n, HD, tokens), BF16),
            pltpu.VMEM((n, HD, tokens), F32),
            pltpu.VMEM((n, HD, tokens), F32),
            pltpu.VMEM((n, 3 * HD, tokens), BF16),
            pltpu.VMEM((n, 3 * HD, tokens), BF16),
            pltpu.VMEM((4 * att, tokens), BF16),
            pltpu.VMEM((width, tokens), F32),
            pltpu.VMEM((width, tokens), BF16),
            pltpu.VMEM((chips * slots, cols), BF16),
            pltpu.VMEM((chips * slots, cols), BF16),
            pltpu.VMEM((parts, rows_dev // 2 // parts, cols), BF16),
            pltpu.VMEM((parts, rows_dev // 2 // parts, cols), BF16),
            dma((4,)),
            dma((2,)),
            dma((2,)),
            dma((2,)),
            dma((5, n)),
            dma((5, n)),
            dma((2,)),
            dma((parts,)),
            dma((parts,)),
            dma((4, parts)),
            dma((4, parts)),
            dma((chips, parts)),
            dma((chips, parts)),
        ],
        compiler_params=pltpu.CompilerParams(
            collective_id=0, has_side_effects=True, vmem_limit_bytes=52 * MIB
        ),
    )(table, accum, ids, lengths, w_uvqk, w_out, cotangent)


def local(table, accum, ids, lengths, w_uvqk, w_out, cotangent):
    n_wide = lax.axis_size("wide")
    n_narrow = lax.axis_size("narrow")
    width = table.shape[1]
    tokens = ids.shape[1]
    output, new_table, new_accum = run_step(
        n_wide,
        n_narrow,
        table,
        accum.reshape(-1, 128),
        ids,
        lengths,
        w_uvqk,
        w_out,
        cotangent.reshape(tokens, width),
    )
    return (output.reshape(1, tokens, width), new_table, new_accum.reshape(accum.shape))


def solution(mesh):
    in_specs = (
        P("wide", None),
        P("wide"),
        P("wide", "narrow"),
        P("wide"),
        P(),
        P(),
        P("wide", "narrow", None),
    )
    out_specs = (P("wide", "narrow", None), P("wide", None), P("wide"))
    return jax.shard_map(local, mesh=mesh, in_specs=in_specs, out_specs=out_specs, check_vma=False)
```

```python
import functools

import jax
import jax.numpy as jnp
from jax import lax
from jax.experimental import pallas as pl
from jax.experimental.pallas import tpu as pltpu
from jax.sharding import PartitionSpec as P

HEADS = 8
HD = 64
CAP = 16
EPS = 1e-05
RATE = 0.5
MESH = pl.DeviceIdType.MESH
F32 = jnp.float32
BF16 = jnp.bfloat16
MIB = 1 << 20
Z = 8
X = 4
DZ = (4, 3, 5, 2, 6, 1, 7, 0)
DX = (2, 1, 3, 0)
DY = (2, 1, 3, 0)
AROUND = [(dz, dx) for dx in DX for dz in DZ]

NN = (((1,), (0,)), ((), ()))
NT = (((1,), (1,)), ((), ()))
TN = (((0,), (0,)), ((), ()))


def mm(a, b, dims=NN):
    return lax.dot_general(a, b, dims, preferred_element_type=F32)


def iota(shape, dim):
    return lax.broadcasted_iota(jnp.int32, shape, dim)


def sigmoid(t):
    return 0.5 * jnp.tanh(0.5 * t) + 0.5


def silu(t):
    return t * sigmoid(t)


def silu_slope(t):
    s = sigmoid(t)
    return s * (1.0 + t * (1.0 - s))


def norm_back(grad, normed, inverse):
    return inverse * (
        grad
        - jnp.mean(grad, axis=0, keepdims=True)
        - normed * jnp.mean(grad * normed, axis=0, keepdims=True)
    )


def onehot(match):
    return match.astype(F32).astype(BF16)


def each(lower, upper, act):
    def step(k, carry):
        act(k)
        return carry

    lax.fori_loop(lower, upper, step, 0)


def remote(src, dst, send_sem, recv_sem, peer):
    return pltpu.make_async_remote_copy(
        src_ref=src,
        dst_ref=dst,
        send_sem=send_sem,
        recv_sem=recv_sem,
        device_id=peer,
        device_id_type=MESH,
    )


def wait_bytes(ref, sem):
    pltpu.make_async_copy(ref, ref, sem).wait()


def tile16(start):
    return pl.ds(pl.multiple_of(start, CAP), CAP)


def step_kernel(
    n_wide, n, table_ref, accum_ref, ids_ref, len_ref, w_hbm, wo_hbm, cot_hbm,
    out_ref, new_table_ref, new_accum_ref, sum_ref,
    tab, w_ref, wo_ref, cot_ref, wt, asks, asked, reply, replies, lanes, hot,
    emb, hid, normed1, qk_out, qk, v_out, v_in, keys, vals, wts, slopes, heads_out, heads, gm, gu,
    gatt_out, gatt, dk, dv, back_out, back, gh, up_t, ge, outgoing, arriving, sib_out, sib_in,
    load_sem, ask_sem, reply_sem, lane_sem, nss, nrs, give_sem, sib_ss, sib_rs, ring_ss, ring_rs,
    pass_ss, pass_rs,
):
    wide = lax.axis_index("wide")
    me = lax.axis_index("narrow")
    chip = me // 2
    core = lax.rem(me, 2)
    chips = n // 2
    rows_dev, width = table_ref.shape
    tokens = ids_ref.shape[1]
    att = HEADS * HD
    slots = n_wide * CAP
    cols = width // chips

    depth, across = wide // X, lax.rem(wide, X)
    zs = [lax.rem(depth + d, Z) * X for d in range(Z)]
    xs = [lax.rem(across + d, X) for d in range(X)]
    ys = [lax.rem(chip + d, chips) for d in range(chips)]

    def far(dz, dx):
        return zs[dz] + xs[dx]

    loads = [
        pltpu.make_async_copy(src, dst, load_sem.at[i])
        for i, (src, dst) in enumerate(
            ((table_ref, tab), (w_hbm, w_ref), (wo_hbm, wo_ref), (cot_hbm, cot_ref))
        )
    ]
    for load in loads:
        load.start()

    finish = []
    barrier = pltpu.get_barrier_semaphore()

    def hail(peer):
        pl.semaphore_signal(barrier, inc=1, device_id=peer, device_id_type=MESH)

    for dz, dx in AROUND[:-1]:
        hail({"wide": far(dz, dx)})
    for k in range(1, n):
        hail({"narrow": lax.rem(me + k, n)})

    ids = ids_ref[...]
    bits = rows_dev.bit_length() - 1
    owner = lax.shift_right_logical(ids, bits)
    row = ids - owner * rows_dev
    hits_f = (owner == iota((n_wide, tokens), 0)).astype(F32)
    before = onehot(iota((tokens, tokens), 0) < iota((tokens, tokens), 1))
    earlier = mm(hits_f.astype(BF16), before)
    slot = jnp.sum(earlier * hits_f, axis=0, keepdims=True).astype(jnp.int32)
    target = owner * CAP + slot
    place = slot + CAP * lax.rem(wide, 8)
    at_place = onehot(place == iota((128, tokens), 0))
    high = lax.shift_right_logical(row, 8)
    low = row - high * 256
    high_m = (hits_f * high.astype(F32)).astype(BF16)
    low_m = (hits_f * low.astype(F32)).astype(BF16)
    wanted = (mm(high_m, at_place, NT) * 256.0 + mm(low_m, at_place, NT)).astype(jnp.int32)
    for o in range(n_wide):
        asks[o] = wanted[o : o + 1, :]

    pl.semaphore_wait(barrier, n_wide - 1 + n - 1)

    for dz, dx in AROUND[:-1]:
        peer = far(dz, dx)
        remote(
            asks.at[peer], asked.at[wide], ask_sem.at[0], ask_sem.at[1], {"wide": peer}
        ).start()
    finish.append(lambda: wait_bytes(asks.at[pl.ds(0, n_wide - 1)], ask_sem.at[0]))
    asked[wide] = asks[wide]
    loads[0].wait()
    wt[...] = tab[...].astype(BF16)
    wait_bytes(asked.at[pl.ds(0, n_wide - 1)], ask_sem.at[1])

    lane16 = iota((CAP, 128), 1)
    sub16 = iota((CAP, 128), 0)
    row_iota = iota((CAP, rows_dev), 1)

    half = n_wide // 4
    for part in range(4):
        for k in range(part * half, (part + 1) * half):
            peer = far(*AROUND[k])
            line = jnp.broadcast_to(asked[peer], (CAP, 128)).astype(F32)
            mine = lane16 == sub16 + CAP * lax.rem(peer, 8)
            column = jnp.sum(jnp.where(mine, line, 0.0), axis=1, keepdims=True).astype(jnp.int32)
            hot[CAP * k : CAP * (k + 1), :] = onehot(column == row_iota)
        lo = part * half * CAP
        reply[lo : lo + half * CAP, :] = mm(hot[lo : lo + half * CAP, :], wt[...]).astype(BF16)
        for k in range(part * half, min((part + 1) * half, n_wide - 1)):
            remote(
                reply.at[pl.ds(k * CAP, CAP)],
                replies.at[tile16(wide * CAP)],
                reply_sem.at[0],
                reply_sem.at[1],
                {"wide": far(*AROUND[k])},
            ).start()
    replies[tile16(wide * CAP), :] = reply[slots - CAP :, :]
    finish.append(lambda: wait_bytes(reply.at[pl.ds(0, slots - CAP)], reply_sem.at[0]))

    for g in range(n_wide // 8):
        total = asked[8 * g]
        for j in range(1, 8):
            total = total + asked[8 * g + j]
        lanes[chip, g : g + 1, :] = total
    for k in range(1, chips):
        remote(
            lanes.at[chip], lanes.at[chip], lane_sem.at[0], lane_sem.at[1],
            {"narrow": ys[k] * 2 + core},
        ).start()
    finish.append(lambda: wait_bytes(lanes.at[pl.ds(0, chips - 1)], lane_sem.at[0]))

    target_t = jnp.transpose(jnp.broadcast_to(target.astype(F32), (128, tokens))).astype(jnp.int32)
    take = jnp.concatenate(
        [onehot(target_t == iota((tokens, 128), 1) + 128 * g) for g in range(slots // 128)],
        axis=1,
    )

    length = len_ref[0]
    live = iota((tokens, 1), 0) + me * tokens < length
    live_t = iota((1, tokens), 1) + me * tokens < length
    for load in loads[1:]:
        load.wait()
    chunk = 256
    eye = onehot(iota((chunk, chunk), 0) == iota((chunk, chunk), 1))
    total_w = w_ref.shape[1]
    for c in range(total_w // chunk):
        part = slice(c * chunk, (c + 1) * chunk)
        wt[part, :] = mm(eye, w_ref[:, part], NT).astype(BF16)
    upstream = jnp.where(live, cot_ref[...], jnp.zeros((), BF16))
    gm[...] = mm(wo_ref[...], upstream, NT)
    up_t[...] = jnp.transpose(upstream.astype(F32))
    wait_bytes(lanes.at[pl.ds(0, chips - 1)], lane_sem.at[1])
    for y in range(chips):
        for g in range(slots // 128):
            lo = y * slots + 128 * g
            hot[:, lo : lo + 128] = onehot(iota((rows_dev, 128), 0) == lanes[y, g : g + 1, :])
    wait_bytes(replies.at[pl.ds(0, slots - CAP)], reply_sem.at[1])
    emb[...] = mm(take, replies[...])

    def exchange(step, source, landing, peer):
        return remote(
            source.at[peer],
            landing.at[me],
            nss.at[step, peer],
            nrs.at[step, me],
            {"narrow": peer},
        )

    def arrive(step, landing, peer):
        wait_bytes(landing.at[peer], nrs.at[step, peer])

    def sent(step, source):
        def one(k):
            peer = lax.rem(me + k, n)
            wait_bytes(source.at[peer], nss.at[step, peer])

        return lambda: each(1, n, one)

    emb_t = jnp.transpose(emb[...])
    center = emb_t - jnp.mean(emb_t, axis=0, keepdims=True)
    inverse1 = lax.rsqrt(jnp.mean(center * center, axis=0, keepdims=True) + EPS)
    normed = center * inverse1
    normed1[...] = normed
    normed_b = normed.astype(BF16)
    for c in range(att // chunk, total_w // chunk):
        hid[c * chunk : (c + 1) * chunk, :] = mm(wt[c * chunk : (c + 1) * chunk, :], normed_b)

    def send_head(k):
        peer = lax.rem(me + k, n)
        base = pl.multiple_of(att + 3 * HD * peer, HD)
        qk_out[peer] = silu(hid[pl.ds(base + HD, 2 * HD), :]).astype(BF16)
        exchange(0, qk_out, qk, peer).start()

    def send_values(k):
        peer = lax.rem(me + k, n)
        base = pl.multiple_of(att + 3 * HD * peer, HD)
        v_out[peer] = hid[pl.ds(base, HD), :].astype(BF16)
        exchange(4, v_out, v_in, peer).start()

    each(1, n, send_head)
    each(1, n, send_values)
    finish.append(sent(0, qk_out))
    finish.append(sent(4, v_out))
    base = pl.multiple_of(att + 3 * HD * me, HD)
    qk[me] = silu(hid[pl.ds(base + HD, 2 * HD), :]).astype(BF16)
    v_in[me] = hid[pl.ds(base, HD), :].astype(BF16)

    for c in range(att // chunk):
        hid[c * chunk : (c + 1) * chunk, :] = mm(wt[c * chunk : (c + 1) * chunk, :], normed_b)
    each(1, n, lambda k: arrive(0, qk, lax.rem(me + k, n)))

    scale = HD**-0.5
    for b in range(n):
        keys[b] = jnp.transpose(qk[b, HD:, :].astype(F32)).astype(BF16)
    causal = iota((tokens, tokens), 0) <= iota((tokens, tokens), 1)

    def tri(j, i):
        return i * (i + 1) // 2 + j

    def weigh(j, i, query):
        score = mm(keys[j], query)
        twice = 1.0 + jnp.tanh(score)
        weight = score * twice
        slope = twice + weight * (2.0 - twice)
        if i == j:
            weight = jnp.where(causal, weight, 0.0)
            slope = jnp.where(causal, slope, 0.0)
        weight = weight.astype(BF16)
        wts[tri(j, i)] = weight
        slopes[tri(j, i)] = slope.astype(BF16)
        return weight

    def send_block(step, source, landing, i):
        @pl.when(i != me)
        def _():
            exchange(step, source, landing, i).start()

        @pl.when(i == me)
        def _():
            landing[i] = source[i]

    early = 3
    for i in range(n - 1, n - 1 - early, -1):
        query = qk[i, :HD, :] * (0.5 * scale)
        for j in range(i + 1):
            weigh(j, i, query)
    each(1, n, lambda k: arrive(4, v_in, lax.rem(me + k, n)))
    for i in reversed(range(n)):
        query = qk[i, :HD, :] * (0.5 * scale)
        attended = jnp.zeros((HD, tokens), F32)
        for j in range(i + 1):
            weight = weigh(j, i, query) if i < n - early else wts[tri(j, i)]
            attended = attended + mm(v_in[j], weight)
        heads_out[i] = attended.astype(BF16)
        send_block(1, heads_out, heads, i)
    for b in range(n):
        vals[b] = jnp.transpose(v_in[b].astype(F32)).astype(BF16)

    finish.append(sent(1, heads_out))
    each(1, n, lambda k: arrive(1, heads, lax.rem(me + k, n)))

    merged = heads[...].astype(F32).reshape(att, tokens)
    center = merged - jnp.mean(merged, axis=0, keepdims=True)
    inverse2 = lax.rsqrt(jnp.mean(center * center, axis=0, keepdims=True) + EPS)
    normed2 = center * inverse2
    gate = silu(hid[:att, :]).astype(BF16).astype(F32)
    grad_mixed = gm[...]
    gu[...] = grad_mixed * normed2
    grad_att = norm_back(grad_mixed * gate, normed2, inverse2).astype(BF16)
    gatt_out[...] = grad_att.reshape(n, HD, tokens)
    each(1, n, lambda k: exchange(2, gatt_out, gatt, lax.rem(me + k, n)).start())
    finish.append(sent(2, gatt_out))
    gatt[me] = gatt_out[me]
    mixed = jnp.transpose(normed2 * gate).astype(BF16)
    result = emb[...] + mm(mixed, wo_ref[...])
    out_ref[...] = jnp.where(live, result, 0.0).astype(BF16)
    gh[:att, :] = (gu[...] * silu_slope(hid[:att, :])).astype(BF16)
    dk[...] = jnp.zeros_like(dk)
    dv[...] = jnp.zeros_like(dv)

    for i in reversed(range(n)):

        @pl.when(i != me)
        def _():
            arrive(2, gatt, i)

        grad = gatt[i]
        query = qk[i, :HD, :]
        dq = jnp.zeros((HD, tokens), F32)
        for j in range(i + 1):
            dw = mm(vals[j], grad)
            ds = (dw * slopes[tri(j, i)].astype(F32)).astype(BF16)
            dv[j] += mm(grad, wts[tri(j, i)], NT)
            dk[j] += mm(query, ds, NT)
            dq = dq + mm(qk[j, HD:, :], ds)
        back_out[i, :HD, :] = dv[i].astype(BF16)
        back_out[i, HD : 2 * HD, :] = (dq * (0.5 * scale)).astype(BF16)
        back_out[i, 2 * HD :, :] = (dk[i] * (0.5 * scale)).astype(BF16)
        send_block(3, back_out, back, i)

    finish.append(sent(3, back_out))
    hid[att:, :] = silu_slope(hid[att:, :])
    put = onehot(iota((slots, tokens), 0) == target)
    each(1, n, lambda k: arrive(3, back, lax.rem(me + k, n)))
    for h in range(HEADS):
        base = att + 3 * HD * h
        gh[base : base + HD, :] = back[h, :HD, :]
        gh[base + HD : base + 3 * HD, :] = (
            back[h, HD:, :].astype(F32) * hid[base + HD : base + 3 * HD, :]
        ).astype(BF16)
    grad_norm1 = mm(w_ref[...], gh[...])
    grad_emb = norm_back(grad_norm1, normed1[...], inverse1) + up_t[...]
    ge[...] = jnp.where(live_t, grad_emb, 0.0).astype(BF16)

    own = tile16(chip * slots + wide * CAP)

    for dy in DY:
        y = ys[dy]
        block = ge[pl.ds(pl.multiple_of(y * cols, cols), cols), :]
        outgoing[pl.ds(pl.multiple_of(y * slots, slots), slots), :] = mm(put, block, NT).astype(BF16)
        for dz, dx in AROUND:
            if dz or dx or dy:
                o = far(dz, dx)
                remote(
                    outgoing.at[tile16(y * slots + o * CAP)],
                    arriving.at[own],
                    give_sem.at[0],
                    give_sem.at[1],
                    {"wide": o, "narrow": y * 2 + core},
                ).start()
    finish.append(lambda: wait_bytes(outgoing.at[pl.ds(0, chips * slots - CAP)], give_sem.at[0]))
    arriving[own, :] = outgoing[own, :]
    wait_bytes(arriving.at[pl.ds(0, chips * slots - CAP)], give_sem.at[1])

    half_rows = rows_dev // 2
    parts = 4
    piece = half_rows // parts
    sibling = {"narrow": chip * 2 + 1 - core}

    def rows_at(side, p):
        return pl.ds(pl.multiple_of(side * half_rows + p * piece, piece), piece)

    def swap(p):
        return remote(sib_out.at[p], sib_in.at[p], sib_ss.at[p], sib_rs.at[p], sibling)

    def ring(way, hop, p):
        spot = sum_ref.at[ys[(1 - hop) * way % chips], rows_at(core, p)]
        lane = 2 * hop - 2 + (way < 0)
        return remote(
            spot, spot, ring_ss.at[lane, p], ring_rs.at[lane, p], {"narrow": ys[way % chips] * 2 + core}
        )

    def pass_on(k, p):
        spot = sum_ref.at[ys[k], rows_at(core, p)]
        return remote(spot, spot, pass_ss.at[k, p], pass_rs.at[k, p], sibling)

    groups = piece // 128

    def update(side, p):
        first = side * (half_rows // 128) + p * groups
        for g in range(groups):
            part = pl.ds(pl.multiple_of(side * half_rows + p * piece + g * 128, 128), 128)
            grads = [sum_ref[y, part, :].astype(F32) for y in range(chips)]
            square = sum(v * v for v in grads)
            mean = jnp.sum(square, axis=1, keepdims=True) * (1.0 / width)
            line = jnp.transpose(jnp.broadcast_to(mean, (128, 128)))[:1, :]
            spot = pl.ds(first + g, 1)
            accum = accum_ref[spot, :] + line
            new_accum_ref[spot, :] = accum
            factor = jnp.transpose(jnp.broadcast_to(RATE * lax.rsqrt(accum), (128, 128)))
            for y in range(chips):
                lane = slice(y * cols, (y + 1) * cols)
                new_table_ref[part, lane] = tab[part, lane] - grads[y] * factor

    low, high = tuple(range(parts // 2)), tuple(range(parts // 2, parts))
    order = [p for pair in zip(low, high) for p in pair]

    def offer(p):
        sib_out[p] = mm(hot[rows_at(1 - core, p), :], arriving[...]).astype(BF16)
        swap(p).start()

    offer(order[0])
    for at, p in enumerate(order):
        if at + 1 < parts:
            offer(order[at + 1])
        total = mm(hot[rows_at(core, p), :], arriving[...])
        swap(p).wait_recv()
        sum_ref[chip, rows_at(core, p), :] = (total + sib_in[p].astype(F32)).astype(BF16)
        ring(1 if p in low else -1, 1, p).start()
        pass_on(0, p).start()
    for p in order:
        ring(-1 if p in low else 1, 1, p).start()
    for p in order:
        way = 1 if p in low else -1
        ring(way, 1, p).wait_recv()
        ring(way, 2, p).start()
        pass_on(-way % chips, p).start()
    for at, p in enumerate(order):
        way = 1 if p in low else -1
        ring(-way, 1, p).wait_recv()
        pass_on(way % chips, p).start()
    for at, p in enumerate(order):
        way = 1 if p in low else -1
        ring(way, 2, p).wait_recv()
        pass_on(2, p).start()
        update(core, p)
        if at:
            q = order[at - 1]
            for k in range(chips):
                pass_on(k, q).wait_recv()
            update(1 - core, q)
    for k in range(chips):
        pass_on(k, order[-1]).wait_recv()
    update(1 - core, order[-1])

    for wait in finish:
        wait()
    for p in range(parts):
        swap(p).wait_send()
        for way in (1, -1):
            ring(way, 1, p).wait_send()
        ring(1 if p in low else -1, 2, p).wait_send()
        for k in range(chips):
            pass_on(k, p).wait_send()


def run_step(n_wide, n, table, accum, ids, lengths, w_uvqk, w_out, cotangent):
    rows_dev, width = table.shape
    tokens = ids.shape[1]
    att = HEADS * HD
    chips = n // 2
    slots = n_wide * CAP
    cols = width // chips
    parts = 4
    vmem = pl.BlockSpec(memory_space=pltpu.VMEM)
    hbm = pl.BlockSpec(memory_space=pltpu.HBM)
    dma = pltpu.SemaphoreType.DMA
    return pl.pallas_call(
        functools.partial(step_kernel, n_wide, n),
        out_shape=(
            pltpu.VMEM((tokens, width), BF16),
            pltpu.VMEM((rows_dev, width), F32),
            pltpu.VMEM((rows_dev // 128, 128), F32),
        ),
        in_specs=[hbm, vmem, vmem, pl.BlockSpec(memory_space=pltpu.SMEM), hbm, hbm, hbm],
        out_specs=(vmem, vmem, vmem),
        scratch_shapes=[
            pltpu.VMEM((chips, rows_dev, cols), BF16),
            pltpu.VMEM((rows_dev, width), F32),
            pltpu.VMEM(w_uvqk.shape, BF16),
            pltpu.VMEM(w_out.shape, BF16),
            pltpu.VMEM((tokens, width), BF16),
            pltpu.VMEM((w_uvqk.shape[1], width), BF16),
            pltpu.VMEM((n_wide, 1, 128), jnp.int32),
            pltpu.VMEM((n_wide, 1, 128), jnp.int32),
            pltpu.VMEM((slots, width), BF16),
            pltpu.VMEM((slots, width), BF16),
            pltpu.VMEM((chips, n_wide // 8, 128), jnp.int32),
            pltpu.VMEM((rows_dev, chips * slots), BF16),
            pltpu.VMEM((tokens, width), F32),
            pltpu.VMEM((4 * att, tokens), F32),
            pltpu.VMEM((width, tokens), F32),
            pltpu.VMEM((n, 2 * HD, tokens), BF16),
            pltpu.VMEM((n, 2 * HD, tokens), BF16),
            pltpu.VMEM((n, HD, tokens), BF16),
            pltpu.VMEM((n, HD, tokens), BF16),
            pltpu.VMEM((n, tokens, HD), BF16),
            pltpu.VMEM((n, tokens, HD), BF16),
            pltpu.VMEM((n * (n + 1) // 2, tokens, tokens), BF16),
            pltpu.VMEM((n * (n + 1) // 2, tokens, tokens), BF16),
            pltpu.VMEM((n, HD, tokens), BF16),
            pltpu.VMEM((n, HD, tokens), BF16),
            pltpu.VMEM((att, tokens), F32),
            pltpu.VMEM((att, tokens), F32),
            pltpu.VMEM((n, HD, tokens), BF16),
            pltpu.VMEM((n, HD, tokens), BF16),
            pltpu.VMEM((n, HD, tokens), F32),
            pltpu.VMEM((n, HD, tokens), F32),
            pltpu.VMEM((n, 3 * HD, tokens), BF16),
            pltpu.VMEM((n, 3 * HD, tokens), BF16),
            pltpu.VMEM((4 * att, tokens), BF16),
            pltpu.VMEM((width, tokens), F32),
            pltpu.VMEM((width, tokens), BF16),
            pltpu.VMEM((chips * slots, cols), BF16),
            pltpu.VMEM((chips * slots, cols), BF16),
            pltpu.VMEM((parts, rows_dev // 2 // parts, cols), BF16),
            pltpu.VMEM((parts, rows_dev // 2 // parts, cols), BF16),
            dma((4,)),
            dma((2,)),
            dma((2,)),
            dma((2,)),
            dma((5, n)),
            dma((5, n)),
            dma((2,)),
            dma((parts,)),
            dma((parts,)),
            dma((4, parts)),
            dma((4, parts)),
            dma((chips, parts)),
            dma((chips, parts)),
        ],
        compiler_params=pltpu.CompilerParams(
            collective_id=0, has_side_effects=True, vmem_limit_bytes=52 * MIB
        ),
    )(table, accum, ids, lengths, w_uvqk, w_out, cotangent)


def local(table, accum, ids, lengths, w_uvqk, w_out, cotangent):
    n_wide = lax.axis_size("wide")
    n_narrow = lax.axis_size("narrow")
    width = table.shape[1]
    tokens = ids.shape[1]
    output, new_table, new_accum = run_step(
        n_wide,
        n_narrow,
        table,
        accum.reshape(-1, 128),
        ids,
        lengths,
        w_uvqk,
        w_out,
        cotangent.reshape(tokens, width),
    )
    return (output.reshape(1, tokens, width), new_table, new_accum.reshape(accum.shape))


def solution(mesh):
    in_specs = (
        P("wide", None),
        P("wide"),
        P("wide", "narrow"),
        P("wide"),
        P(),
        P(),
        P("wide", "narrow", None),
    )
    out_specs = (P("wide", "narrow", None), P("wide", None), P("wide"))
    return jax.shard_map(local, mesh=mesh, in_specs=in_specs, out_specs=out_specs, check_vma=False)
```

```python
import functools

import jax
import jax.numpy as jnp
from jax import lax
from jax.experimental import pallas as pl
from jax.experimental.pallas import tpu as pltpu
from jax.sharding import PartitionSpec as P

HEADS = 8
HD = 64
CAP = 16
EPS = 1e-05
RATE = 0.5
MESH = pl.DeviceIdType.MESH
F32 = jnp.float32
BF16 = jnp.bfloat16
MIB = 1 << 20
Z = 8
X = 4
DZ = (4, 3, 5, 2, 6, 1, 7, 0)
DX = (2, 1, 3, 0)
DY = (2, 1, 3, 0)
AROUND = [(dz, dx) for dx in DX for dz in DZ]

NN = (((1,), (0,)), ((), ()))
NT = (((1,), (1,)), ((), ()))
TN = (((0,), (0,)), ((), ()))


def mm(a, b, dims=NN):
    return lax.dot_general(a, b, dims, preferred_element_type=F32)


def iota(shape, dim):
    return lax.broadcasted_iota(jnp.int32, shape, dim)


def sigmoid(t):
    return 0.5 * jnp.tanh(0.5 * t) + 0.5


def silu(t):
    return t * sigmoid(t)


def silu_slope(t):
    s = sigmoid(t)
    return s * (1.0 + t * (1.0 - s))


def norm_back(grad, normed, inverse):
    return inverse * (
        grad
        - jnp.mean(grad, axis=0, keepdims=True)
        - normed * jnp.mean(grad * normed, axis=0, keepdims=True)
    )


def onehot(match):
    return match.astype(F32).astype(BF16)


def each(lower, upper, act):
    def step(k, carry):
        act(k)
        return carry

    lax.fori_loop(lower, upper, step, 0)


def remote(src, dst, send_sem, recv_sem, peer):
    return pltpu.make_async_remote_copy(
        src_ref=src,
        dst_ref=dst,
        send_sem=send_sem,
        recv_sem=recv_sem,
        device_id=peer,
        device_id_type=MESH,
    )


def wait_bytes(ref, sem):
    pltpu.make_async_copy(ref, ref, sem).wait()


def tile16(start):
    return pl.ds(pl.multiple_of(start, CAP), CAP)


def step_kernel(
    n_wide, n, table_ref, accum_ref, ids_ref, len_ref, w_hbm, wo_hbm, cot_hbm,
    out_ref, new_table_ref, new_accum_ref, sum_ref,
    tab, w_ref, wo_ref, cot_ref, wt, asks, asked, reply, replies, lanes, hot,
    emb, hid, normed1, qk_out, qk, v_out, v_in, keys, vals, wts, slopes, heads_out, heads, gm, gu, gates, gn,
    gatt_out, gatt, dk, dv, back_out, back, gh, up_t, ge, outgoing, arriving, sib_out, sib_in,
    load_sem, ask_sem, reply_sem, lane_sem, nss, nrs, give_sem, sib_ss, sib_rs, ring_ss, ring_rs,
    pass_ss, pass_rs,
):
    wide = lax.axis_index("wide")
    me = lax.axis_index("narrow")
    chip = me // 2
    core = lax.rem(me, 2)
    chips = n // 2
    rows_dev, width = table_ref.shape
    tokens = ids_ref.shape[1]
    att = HEADS * HD
    slots = n_wide * CAP
    cols = width // chips

    depth, across = wide // X, lax.rem(wide, X)
    zs = [lax.rem(depth + d, Z) * X for d in range(Z)]
    xs = [lax.rem(across + d, X) for d in range(X)]
    ys = [lax.rem(chip + d, chips) for d in range(chips)]

    def far(dz, dx):
        return zs[dz] + xs[dx]

    loads = [
        pltpu.make_async_copy(src, dst, load_sem.at[i])
        for i, (src, dst) in enumerate(
            ((table_ref, tab), (w_hbm, w_ref), (wo_hbm, wo_ref), (cot_hbm, cot_ref))
        )
    ]
    for load in loads:
        load.start()

    finish = []
    barrier = pltpu.get_barrier_semaphore()

    def hail(peer):
        pl.semaphore_signal(barrier, inc=1, device_id=peer, device_id_type=MESH)

    for dz, dx in AROUND[:-1]:
        hail({"wide": far(dz, dx)})
    for k in range(1, n):
        hail({"narrow": lax.rem(me + k, n)})

    ids = ids_ref[...]
    bits = rows_dev.bit_length() - 1
    owner = lax.shift_right_logical(ids, bits)
    row = ids - owner * rows_dev
    hits_f = (owner == iota((n_wide, tokens), 0)).astype(F32)
    before = onehot(iota((tokens, tokens), 0) < iota((tokens, tokens), 1))
    earlier = mm(hits_f.astype(BF16), before)
    slot = jnp.sum(earlier * hits_f, axis=0, keepdims=True).astype(jnp.int32)
    target = owner * CAP + slot
    place = slot + CAP * lax.rem(wide, 8)
    at_place = onehot(place == iota((128, tokens), 0))
    high = lax.shift_right_logical(row, 8)
    low = row - high * 256
    high_m = (hits_f * high.astype(F32)).astype(BF16)
    low_m = (hits_f * low.astype(F32)).astype(BF16)
    wanted = (mm(high_m, at_place, NT) * 256.0 + mm(low_m, at_place, NT)).astype(jnp.int32)
    for o in range(n_wide):
        asks[o] = wanted[o : o + 1, :]

    pl.semaphore_wait(barrier, n_wide - 1 + n - 1)

    for dz, dx in AROUND[:-1]:
        peer = far(dz, dx)
        remote(
            asks.at[peer], asked.at[wide], ask_sem.at[0], ask_sem.at[1], {"wide": peer}
        ).start()
    finish.append(lambda: wait_bytes(asks.at[pl.ds(0, n_wide - 1)], ask_sem.at[0]))
    asked[wide] = asks[wide]
    loads[0].wait()
    wt[...] = tab[...].astype(BF16)
    wait_bytes(asked.at[pl.ds(0, n_wide - 1)], ask_sem.at[1])

    lane16 = iota((CAP, 128), 1)
    sub16 = iota((CAP, 128), 0)
    row_iota = iota((CAP, rows_dev), 1)

    half = n_wide // 4
    for part in range(4):
        for k in range(part * half, (part + 1) * half):
            peer = far(*AROUND[k])
            line = jnp.broadcast_to(asked[peer], (CAP, 128)).astype(F32)
            mine = lane16 == sub16 + CAP * lax.rem(peer, 8)
            column = jnp.sum(jnp.where(mine, line, 0.0), axis=1, keepdims=True).astype(jnp.int32)
            hot[CAP * k : CAP * (k + 1), :] = onehot(column == row_iota)
        lo = part * half * CAP
        reply[lo : lo + half * CAP, :] = mm(hot[lo : lo + half * CAP, :], wt[...]).astype(BF16)
        for k in range(part * half, min((part + 1) * half, n_wide - 1)):
            remote(
                reply.at[pl.ds(k * CAP, CAP)],
                replies.at[tile16(wide * CAP)],
                reply_sem.at[0],
                reply_sem.at[1],
                {"wide": far(*AROUND[k])},
            ).start()
    replies[tile16(wide * CAP), :] = reply[slots - CAP :, :]
    finish.append(lambda: wait_bytes(reply.at[pl.ds(0, slots - CAP)], reply_sem.at[0]))

    for g in range(n_wide // 8):
        total = asked[8 * g]
        for j in range(1, 8):
            total = total + asked[8 * g + j]
        lanes[chip, g : g + 1, :] = total
    for k in range(1, chips):
        remote(
            lanes.at[chip], lanes.at[chip], lane_sem.at[0], lane_sem.at[1],
            {"narrow": ys[k] * 2 + core},
        ).start()
    finish.append(lambda: wait_bytes(lanes.at[pl.ds(0, chips - 1)], lane_sem.at[0]))

    target_t = jnp.transpose(jnp.broadcast_to(target.astype(F32), (128, tokens))).astype(jnp.int32)
    take = jnp.concatenate(
        [onehot(target_t == iota((tokens, 128), 1) + 128 * g) for g in range(slots // 128)],
        axis=1,
    )

    length = len_ref[0]
    live = iota((tokens, 1), 0) + me * tokens < length
    live_t = iota((1, tokens), 1) + me * tokens < length
    for load in loads[1:]:
        load.wait()
    chunk = 256
    eye = onehot(iota((chunk, chunk), 0) == iota((chunk, chunk), 1))
    total_w = w_ref.shape[1]
    for c in range(total_w // chunk):
        part = slice(c * chunk, (c + 1) * chunk)
        wt[part, :] = mm(eye, w_ref[:, part], NT).astype(BF16)
    upstream = jnp.where(live, cot_ref[...], jnp.zeros((), BF16))
    gm[...] = mm(wo_ref[...], upstream, NT)
    up_t[...] = jnp.transpose(upstream.astype(F32))
    wait_bytes(lanes.at[pl.ds(0, chips - 1)], lane_sem.at[1])
    for y in range(chips):
        for g in range(slots // 128):
            lo = y * slots + 128 * g
            hot[:, lo : lo + 128] = onehot(iota((rows_dev, 128), 0) == lanes[y, g : g + 1, :])
    wait_bytes(replies.at[pl.ds(0, slots - CAP)], reply_sem.at[1])
    emb[...] = mm(take, replies[...])

    def exchange(step, source, landing, peer):
        return remote(
            source.at[peer],
            landing.at[me],
            nss.at[step, peer],
            nrs.at[step, me],
            {"narrow": peer},
        )

    def arrive(step, landing, peer):
        wait_bytes(landing.at[peer], nrs.at[step, peer])

    def sent(step, source):
        def one(k):
            peer = lax.rem(me + k, n)
            wait_bytes(source.at[peer], nss.at[step, peer])

        return lambda: each(1, n, one)

    emb_t = jnp.transpose(emb[...])
    center = emb_t - jnp.mean(emb_t, axis=0, keepdims=True)
    inverse1 = lax.rsqrt(jnp.mean(center * center, axis=0, keepdims=True) + EPS)
    normed = center * inverse1
    normed1[...] = normed
    normed_b = normed.astype(BF16)
    for c in range(att // chunk, total_w // chunk):
        hid[c * chunk : (c + 1) * chunk, :] = mm(wt[c * chunk : (c + 1) * chunk, :], normed_b)

    near = [me, chip * 2 + 1 - core]
    near += [ys[dy] * 2 + c for dy in (1, 3) for c in (core, 1 - core)]
    near += [ys[2] * 2 + c for c in (core, 1 - core)]

    for peer in near[1:]:
        base = pl.multiple_of(att + 3 * HD * peer, HD)
        qk_out[peer] = silu(hid[pl.ds(base + HD, 2 * HD), :]).astype(BF16)
        exchange(0, qk_out, qk, peer).start()
    for peer in near[1:]:
        base = pl.multiple_of(att + 3 * HD * peer, HD)
        v_out[peer] = hid[pl.ds(base, HD), :].astype(BF16)
        exchange(4, v_out, v_in, peer).start()
    finish.append(sent(0, qk_out))
    finish.append(sent(4, v_out))
    base = pl.multiple_of(att + 3 * HD * me, HD)
    qk[me] = silu(hid[pl.ds(base + HD, 2 * HD), :]).astype(BF16)
    v_in[me] = hid[pl.ds(base, HD), :].astype(BF16)

    for c in range(att // chunk):
        hid[c * chunk : (c + 1) * chunk, :] = mm(wt[c * chunk : (c + 1) * chunk, :], normed_b)
    gate = hid[:att, :]
    gates[...] = silu(gate).astype(BF16).astype(F32)
    gn[...] = gm[...] * gates[...]
    gu[...] = silu_slope(gate)

    scale = HD**-0.5
    causal = iota((tokens, tokens), 0) <= iota((tokens, tokens), 1)

    def tri(j, i):
        return i * (i + 1) // 2 + j

    def weigh(j, i, diagonal):
        score = mm(keys[j], qk[i, :HD, :] * (0.5 * scale))
        twice = 1.0 + jnp.tanh(score)
        weight = score * twice
        slope = twice + weight * (2.0 - twice)
        if diagonal:
            weight = jnp.where(causal, weight, 0.0)
            slope = jnp.where(causal, slope, 0.0)
        wts[tri(j, i)] = weight.astype(BF16)
        slopes[tri(j, i)] = slope.astype(BF16)

    for at, here in enumerate(near):
        if at:
            arrive(0, qk, here)
        keys[here] = jnp.transpose(qk[here, HD:, :].astype(F32)).astype(BF16)
        for other in near[:at]:
            later = (here + n - other) // n
            weigh(here + later * (other - here), other + later * (here - other), False)
        weigh(here, here, True)

    def send_block(step, source, landing, i):
        @pl.when(i != me)
        def _():
            exchange(step, source, landing, i).start()

        @pl.when(i == me)
        def _():
            landing[i] = source[i]

    each(1, n, lambda k: arrive(4, v_in, lax.rem(me + k, n)))
    for i in reversed(range(n)):
        attended = jnp.zeros((HD, tokens), F32)
        for j in range(i + 1):
            attended = attended + mm(v_in[j], wts[tri(j, i)])
        heads_out[i] = attended.astype(BF16)
        send_block(1, heads_out, heads, i)
    for b in range(n):
        vals[b] = jnp.transpose(v_in[b].astype(F32)).astype(BF16)

    finish.append(sent(1, heads_out))
    each(1, n, lambda k: arrive(1, heads, lax.rem(me + k, n)))

    merged = heads[...].astype(F32).reshape(att, tokens)
    center = merged - jnp.mean(merged, axis=0, keepdims=True)
    inverse2 = lax.rsqrt(jnp.mean(center * center, axis=0, keepdims=True) + EPS)
    normed2 = center * inverse2
    grad_att = norm_back(gn[...], normed2, inverse2).astype(BF16)
    gatt_out[...] = grad_att.reshape(n, HD, tokens)
    each(1, n, lambda k: exchange(2, gatt_out, gatt, lax.rem(me + k, n)).start())
    finish.append(sent(2, gatt_out))
    gatt[me] = gatt_out[me]
    mixed = jnp.transpose(normed2 * gates[...]).astype(BF16)
    result = emb[...] + mm(mixed, wo_ref[...])
    out_ref[...] = jnp.where(live, result, 0.0).astype(BF16)
    gh[:att, :] = (gm[...] * normed2 * gu[...]).astype(BF16)
    dk[...] = jnp.zeros_like(dk)
    dv[...] = jnp.zeros_like(dv)

    for i in reversed(range(n)):

        @pl.when(i != me)
        def _():
            arrive(2, gatt, i)

        grad = gatt[i]
        query = qk[i, :HD, :]
        dq = jnp.zeros((HD, tokens), F32)
        for j in range(i + 1):
            dw = mm(vals[j], grad)
            ds = (dw * slopes[tri(j, i)].astype(F32)).astype(BF16)
            dv[j] += mm(grad, wts[tri(j, i)], NT)
            dk[j] += mm(query, ds, NT)
            dq = dq + mm(qk[j, HD:, :], ds)
        back_out[i, :HD, :] = dv[i].astype(BF16)
        back_out[i, HD : 2 * HD, :] = (dq * (0.5 * scale)).astype(BF16)
        back_out[i, 2 * HD :, :] = (dk[i] * (0.5 * scale)).astype(BF16)
        send_block(3, back_out, back, i)

    finish.append(sent(3, back_out))
    hid[att:, :] = silu_slope(hid[att:, :])
    put = onehot(iota((slots, tokens), 0) == target)
    gate_part = mm(w_ref[:, :att], gh[:att, :])
    each(1, n, lambda k: arrive(3, back, lax.rem(me + k, n)))
    for h in range(HEADS):
        base = att + 3 * HD * h
        gh[base : base + HD, :] = back[h, :HD, :]
        gh[base + HD : base + 3 * HD, :] = (
            back[h, HD:, :].astype(F32) * hid[base + HD : base + 3 * HD, :]
        ).astype(BF16)
    grad_norm1 = gate_part + mm(w_ref[:, att:], gh[att:, :])
    grad_emb = norm_back(grad_norm1, normed1[...], inverse1) + up_t[...]
    ge[...] = jnp.where(live_t, grad_emb, 0.0).astype(BF16)

    own = tile16(chip * slots + wide * CAP)

    for dy in DY:
        y = ys[dy]
        block = ge[pl.ds(pl.multiple_of(y * cols, cols), cols), :]
        outgoing[pl.ds(pl.multiple_of(y * slots, slots), slots), :] = mm(put, block, NT).astype(BF16)
        for dz, dx in AROUND:
            if dz or dx or dy:
                o = far(dz, dx)
                remote(
                    outgoing.at[tile16(y * slots + o * CAP)],
                    arriving.at[own],
                    give_sem.at[0],
                    give_sem.at[1],
                    {"wide": o, "narrow": y * 2 + core},
                ).start()
    finish.append(lambda: wait_bytes(outgoing.at[pl.ds(0, chips * slots - CAP)], give_sem.at[0]))
    arriving[own, :] = outgoing[own, :]
    wait_bytes(arriving.at[pl.ds(0, chips * slots - CAP)], give_sem.at[1])

    half_rows = rows_dev // 2
    parts = 4
    piece = half_rows // parts
    sibling = {"narrow": chip * 2 + 1 - core}

    def rows_at(side, p):
        return pl.ds(pl.multiple_of(side * half_rows + p * piece, piece), piece)

    def swap(p):
        return remote(sib_out.at[p], sib_in.at[p], sib_ss.at[p], sib_rs.at[p], sibling)

    def ring(way, hop, p):
        spot = sum_ref.at[ys[(1 - hop) * way % chips], rows_at(core, p)]
        lane = 2 * hop - 2 + (way < 0)
        return remote(
            spot, spot, ring_ss.at[lane, p], ring_rs.at[lane, p], {"narrow": ys[way % chips] * 2 + core}
        )

    def pass_on(k, p):
        spot = sum_ref.at[ys[k], rows_at(core, p)]
        return remote(spot, spot, pass_ss.at[k, p], pass_rs.at[k, p], sibling)

    groups = piece // 128

    def update(side, p):
        first = side * (half_rows // 128) + p * groups
        for g in range(groups):
            part = pl.ds(pl.multiple_of(side * half_rows + p * piece + g * 128, 128), 128)
            grads = [sum_ref[y, part, :].astype(F32) for y in range(chips)]
            square = sum(v * v for v in grads)
            mean = jnp.sum(square, axis=1, keepdims=True) * (1.0 / width)
            line = jnp.transpose(jnp.broadcast_to(mean, (128, 128)))[:1, :]
            spot = pl.ds(first + g, 1)
            accum = accum_ref[spot, :] + line
            new_accum_ref[spot, :] = accum
            factor = jnp.transpose(jnp.broadcast_to(RATE * lax.rsqrt(accum), (128, 128)))
            for y in range(chips):
                lane = slice(y * cols, (y + 1) * cols)
                new_table_ref[part, lane] = tab[part, lane] - grads[y] * factor

    low, high = tuple(range(parts // 2)), tuple(range(parts // 2, parts))
    order = [p for pair in zip(low, high) for p in pair]

    def offer(p):
        sib_out[p] = mm(hot[rows_at(1 - core, p), :], arriving[...]).astype(BF16)
        swap(p).start()

    offer(order[0])
    for at, p in enumerate(order):
        if at + 1 < parts:
            offer(order[at + 1])
        total = mm(hot[rows_at(core, p), :], arriving[...])
        swap(p).wait_recv()
        sum_ref[chip, rows_at(core, p), :] = (total + sib_in[p].astype(F32)).astype(BF16)
        ring(1 if p in low else -1, 1, p).start()
        pass_on(0, p).start()
    for p in order:
        ring(-1 if p in low else 1, 1, p).start()
    for p in order:
        way = 1 if p in low else -1
        ring(way, 1, p).wait_recv()
        ring(way, 2, p).start()
        pass_on(-way % chips, p).start()
    for at, p in enumerate(order):
        way = 1 if p in low else -1
        ring(-way, 1, p).wait_recv()
        pass_on(way % chips, p).start()
    for at, p in enumerate(order):
        way = 1 if p in low else -1
        ring(way, 2, p).wait_recv()
        pass_on(2, p).start()
        update(core, p)
        if at:
            q = order[at - 1]
            for k in range(chips):
                pass_on(k, q).wait_recv()
            update(1 - core, q)
    for k in range(chips):
        pass_on(k, order[-1]).wait_recv()
    update(1 - core, order[-1])

    for wait in finish:
        wait()
    for p in range(parts):
        swap(p).wait_send()
        for way in (1, -1):
            ring(way, 1, p).wait_send()
        ring(1 if p in low else -1, 2, p).wait_send()
        for k in range(chips):
            pass_on(k, p).wait_send()


def run_step(n_wide, n, table, accum, ids, lengths, w_uvqk, w_out, cotangent):
    rows_dev, width = table.shape
    tokens = ids.shape[1]
    att = HEADS * HD
    chips = n // 2
    slots = n_wide * CAP
    cols = width // chips
    parts = 4
    vmem = pl.BlockSpec(memory_space=pltpu.VMEM)
    hbm = pl.BlockSpec(memory_space=pltpu.HBM)
    dma = pltpu.SemaphoreType.DMA
    return pl.pallas_call(
        functools.partial(step_kernel, n_wide, n),
        out_shape=(
            pltpu.VMEM((tokens, width), BF16),
            pltpu.VMEM((rows_dev, width), F32),
            pltpu.VMEM((rows_dev // 128, 128), F32),
        ),
        in_specs=[hbm, vmem, vmem, pl.BlockSpec(memory_space=pltpu.SMEM), hbm, hbm, hbm],
        out_specs=(vmem, vmem, vmem),
        scratch_shapes=[
            pltpu.VMEM((chips, rows_dev, cols), BF16),
            pltpu.VMEM((rows_dev, width), F32),
            pltpu.VMEM(w_uvqk.shape, BF16),
            pltpu.VMEM(w_out.shape, BF16),
            pltpu.VMEM((tokens, width), BF16),
            pltpu.VMEM((w_uvqk.shape[1], width), BF16),
            pltpu.VMEM((n_wide, 1, 128), jnp.int32),
            pltpu.VMEM((n_wide, 1, 128), jnp.int32),
            pltpu.VMEM((slots, width), BF16),
            pltpu.VMEM((slots, width), BF16),
            pltpu.VMEM((chips, n_wide // 8, 128), jnp.int32),
            pltpu.VMEM((rows_dev, chips * slots), BF16),
            pltpu.VMEM((tokens, width), F32),
            pltpu.VMEM((4 * att, tokens), F32),
            pltpu.VMEM((width, tokens), F32),
            pltpu.VMEM((n, 2 * HD, tokens), BF16),
            pltpu.VMEM((n, 2 * HD, tokens), BF16),
            pltpu.VMEM((n, HD, tokens), BF16),
            pltpu.VMEM((n, HD, tokens), BF16),
            pltpu.VMEM((n, tokens, HD), BF16),
            pltpu.VMEM((n, tokens, HD), BF16),
            pltpu.VMEM((n * (n + 1) // 2, tokens, tokens), BF16),
            pltpu.VMEM((n * (n + 1) // 2, tokens, tokens), BF16),
            pltpu.VMEM((n, HD, tokens), BF16),
            pltpu.VMEM((n, HD, tokens), BF16),
            pltpu.VMEM((att, tokens), F32),
            pltpu.VMEM((att, tokens), F32),
            pltpu.VMEM((att, tokens), F32),
            pltpu.VMEM((att, tokens), F32),
            pltpu.VMEM((n, HD, tokens), BF16),
            pltpu.VMEM((n, HD, tokens), BF16),
            pltpu.VMEM((n, HD, tokens), F32),
            pltpu.VMEM((n, HD, tokens), F32),
            pltpu.VMEM((n, 3 * HD, tokens), BF16),
            pltpu.VMEM((n, 3 * HD, tokens), BF16),
            pltpu.VMEM((4 * att, tokens), BF16),
            pltpu.VMEM((width, tokens), F32),
            pltpu.VMEM((width, tokens), BF16),
            pltpu.VMEM((chips * slots, cols), BF16),
            pltpu.VMEM((chips * slots, cols), BF16),
            pltpu.VMEM((parts, rows_dev // 2 // parts, cols), BF16),
            pltpu.VMEM((parts, rows_dev // 2 // parts, cols), BF16),
            dma((4,)),
            dma((2,)),
            dma((2,)),
            dma((2,)),
            dma((5, n)),
            dma((5, n)),
            dma((2,)),
            dma((parts,)),
            dma((parts,)),
            dma((4, parts)),
            dma((4, parts)),
            dma((chips, parts)),
            dma((chips, parts)),
        ],
        compiler_params=pltpu.CompilerParams(
            collective_id=0, has_side_effects=True, vmem_limit_bytes=52 * MIB
        ),
    )(table, accum, ids, lengths, w_uvqk, w_out, cotangent)


def local(table, accum, ids, lengths, w_uvqk, w_out, cotangent):
    n_wide = lax.axis_size("wide")
    n_narrow = lax.axis_size("narrow")
    width = table.shape[1]
    tokens = ids.shape[1]
    output, new_table, new_accum = run_step(
        n_wide,
        n_narrow,
        table,
        accum.reshape(-1, 128),
        ids,
        lengths,
        w_uvqk,
        w_out,
        cotangent.reshape(tokens, width),
    )
    return (output.reshape(1, tokens, width), new_table, new_accum.reshape(accum.shape))


def solution(mesh):
    in_specs = (
        P("wide", None),
        P("wide"),
        P("wide", "narrow"),
        P("wide"),
        P(),
        P(),
        P("wide", "narrow", None),
    )
    out_specs = (P("wide", "narrow", None), P("wide", None), P("wide"))
    return jax.shard_map(local, mesh=mesh, in_specs=in_specs, out_specs=out_specs, check_vma=False)
```

```python
import functools

import jax
import jax.numpy as jnp
from jax import lax
from jax.experimental import pallas as pl
from jax.experimental.pallas import tpu as pltpu
from jax.sharding import PartitionSpec as P

HEADS = 8
HD = 64
CAP = 16
EPS = 1e-05
RATE = 0.5
MESH = pl.DeviceIdType.MESH
F32 = jnp.float32
BF16 = jnp.bfloat16
MIB = 1 << 20
Z = 8
X = 4
DZ = (4, 3, 5, 2, 6, 1, 7, 0)
DX = (2, 1, 3, 0)
DY = (2, 1, 3, 0)
AROUND = [(dz, dx) for dx in DX for dz in DZ]

NN = (((1,), (0,)), ((), ()))
NT = (((1,), (1,)), ((), ()))
TN = (((0,), (0,)), ((), ()))


def mm(a, b, dims=NN):
    return lax.dot_general(a, b, dims, preferred_element_type=F32)


def iota(shape, dim):
    return lax.broadcasted_iota(jnp.int32, shape, dim)


def sigmoid(t):
    return 0.5 * jnp.tanh(0.5 * t) + 0.5


def silu(t):
    return t * sigmoid(t)


def silu_slope(t):
    s = sigmoid(t)
    return s * (1.0 + t * (1.0 - s))


def norm_back(grad, normed, inverse):
    return inverse * (
        grad
        - jnp.mean(grad, axis=0, keepdims=True)
        - normed * jnp.mean(grad * normed, axis=0, keepdims=True)
    )


def onehot(match):
    return match.astype(F32).astype(BF16)


def each(lower, upper, act):
    def step(k, carry):
        act(k)
        return carry

    lax.fori_loop(lower, upper, step, 0)


def remote(src, dst, send_sem, recv_sem, peer):
    return pltpu.make_async_remote_copy(
        src_ref=src,
        dst_ref=dst,
        send_sem=send_sem,
        recv_sem=recv_sem,
        device_id=peer,
        device_id_type=MESH,
    )


def wait_bytes(ref, sem):
    pltpu.make_async_copy(ref, ref, sem).wait()


def tile16(start):
    return pl.ds(pl.multiple_of(start, CAP), CAP)


def step_kernel(
    n_wide, n, table_ref, accum_ref, ids_ref, len_ref, w_hbm, wo_hbm, cot_hbm,
    out_ref, new_table_ref, new_accum_ref, sum_ref,
    tab, w_ref, wo_ref, cot_ref, wt, asks, asked, reply, replies, lanes, hot,
    emb, hid, normed1, qk_out, qk, v_out, v_in, keys, vals, wts, slopes, heads_out, heads, gm, gu, gates, gn,
    gatt_out, gatt, dk, dv, back_out, back, gh, up_t, ge, outgoing, arriving, sib_out, sib_in,
    load_sem, ask_sem, reply_sem, lane_sem, nss, nrs, give_sem, sib_ss, sib_rs, ring_ss, ring_rs,
    pass_ss, pass_rs,
):
    wide = lax.axis_index("wide")
    me = lax.axis_index("narrow")
    chip = me // 2
    core = lax.rem(me, 2)
    chips = n // 2
    rows_dev, width = table_ref.shape
    tokens = ids_ref.shape[1]
    att = HEADS * HD
    slots = n_wide * CAP
    cols = width // chips

    depth, across = wide // X, lax.rem(wide, X)
    zs = [lax.rem(depth + d, Z) * X for d in range(Z)]
    xs = [lax.rem(across + d, X) for d in range(X)]
    ys = [lax.rem(chip + d, chips) for d in range(chips)]

    def far(dz, dx):
        return zs[dz] + xs[dx]

    loads = [
        pltpu.make_async_copy(src, dst, load_sem.at[i])
        for i, (src, dst) in enumerate(
            ((table_ref, tab), (w_hbm, w_ref), (wo_hbm, wo_ref), (cot_hbm, cot_ref))
        )
    ]
    for load in loads:
        load.start()

    finish = []
    barrier = pltpu.get_barrier_semaphore()

    def hail(peer):
        pl.semaphore_signal(barrier, inc=1, device_id=peer, device_id_type=MESH)

    for dz, dx in AROUND[:-1]:
        hail({"wide": far(dz, dx)})
    for k in range(1, n):
        hail({"narrow": lax.rem(me + k, n)})

    ids = ids_ref[...]
    bits = rows_dev.bit_length() - 1
    owner = lax.shift_right_logical(ids, bits)
    row = ids - owner * rows_dev
    hits_f = (owner == iota((n_wide, tokens), 0)).astype(F32)
    before = onehot(iota((tokens, tokens), 0) < iota((tokens, tokens), 1))
    earlier = mm(hits_f.astype(BF16), before)
    slot = jnp.sum(earlier * hits_f, axis=0, keepdims=True).astype(jnp.int32)
    target = owner * CAP + slot
    place = slot + CAP * lax.rem(wide, 8)
    at_place = onehot(place == iota((128, tokens), 0))
    high = lax.shift_right_logical(row, 8)
    low = row - high * 256
    high_m = (hits_f * high.astype(F32)).astype(BF16)
    low_m = (hits_f * low.astype(F32)).astype(BF16)
    wanted = (mm(high_m, at_place, NT) * 256.0 + mm(low_m, at_place, NT)).astype(jnp.int32)
    for o in range(n_wide):
        asks[o] = wanted[o : o + 1, :]

    pl.semaphore_wait(barrier, n_wide - 1 + n - 1)

    for dz, dx in AROUND[:-1]:
        peer = far(dz, dx)
        remote(
            asks.at[peer], asked.at[wide], ask_sem.at[0], ask_sem.at[1], {"wide": peer}
        ).start()
    finish.append(lambda: wait_bytes(asks.at[pl.ds(0, n_wide - 1)], ask_sem.at[0]))
    asked[wide] = asks[wide]
    loads[0].wait()
    wt[...] = tab[...].astype(BF16)
    wait_bytes(asked.at[pl.ds(0, n_wide - 1)], ask_sem.at[1])

    lane16 = iota((CAP, 128), 1)
    sub16 = iota((CAP, 128), 0)
    row_iota = iota((CAP, rows_dev), 1)

    half = n_wide // 4
    for part in range(4):
        for k in range(part * half, (part + 1) * half):
            peer = far(*AROUND[k])
            line = jnp.broadcast_to(asked[peer], (CAP, 128)).astype(F32)
            mine = lane16 == sub16 + CAP * lax.rem(peer, 8)
            column = jnp.sum(jnp.where(mine, line, 0.0), axis=1, keepdims=True).astype(jnp.int32)
            hot[CAP * k : CAP * (k + 1), :] = onehot(column == row_iota)
        lo = part * half * CAP
        reply[lo : lo + half * CAP, :] = mm(hot[lo : lo + half * CAP, :], wt[...]).astype(BF16)
        for k in range(part * half, min((part + 1) * half, n_wide - 1)):
            remote(
                reply.at[pl.ds(k * CAP, CAP)],
                replies.at[tile16(wide * CAP)],
                reply_sem.at[0],
                reply_sem.at[1],
                {"wide": far(*AROUND[k])},
            ).start()
    replies[tile16(wide * CAP), :] = reply[slots - CAP :, :]
    finish.append(lambda: wait_bytes(reply.at[pl.ds(0, slots - CAP)], reply_sem.at[0]))

    for g in range(n_wide // 8):
        total = asked[8 * g]
        for j in range(1, 8):
            total = total + asked[8 * g + j]
        lanes[chip, g : g + 1, :] = total
    for k in range(1, chips):
        remote(
            lanes.at[chip], lanes.at[chip], lane_sem.at[0], lane_sem.at[1],
            {"narrow": ys[k] * 2 + core},
        ).start()
    finish.append(lambda: wait_bytes(lanes.at[pl.ds(0, chips - 1)], lane_sem.at[0]))

    target_t = jnp.transpose(jnp.broadcast_to(target.astype(F32), (128, tokens))).astype(jnp.int32)
    take = jnp.concatenate(
        [onehot(target_t == iota((tokens, 128), 1) + 128 * g) for g in range(slots // 128)],
        axis=1,
    )

    length = len_ref[0]
    live = iota((tokens, 1), 0) + me * tokens < length
    live_t = iota((1, tokens), 1) + me * tokens < length
    for load in loads[1:]:
        load.wait()
    chunk = 256
    eye = onehot(iota((chunk, chunk), 0) == iota((chunk, chunk), 1))
    total_w = w_ref.shape[1]
    for c in range(total_w // chunk):
        part = slice(c * chunk, (c + 1) * chunk)
        wt[part, :] = mm(eye, w_ref[:, part], NT).astype(BF16)
    upstream = jnp.where(live, cot_ref[...], jnp.zeros((), BF16))
    gm[...] = mm(wo_ref[...], upstream, NT)
    up_t[...] = jnp.transpose(upstream.astype(F32))
    wait_bytes(lanes.at[pl.ds(0, chips - 1)], lane_sem.at[1])
    for y in range(chips):
        for g in range(slots // 128):
            lo = y * slots + 128 * g
            hot[:, lo : lo + 128] = onehot(iota((rows_dev, 128), 0) == lanes[y, g : g + 1, :])
    wait_bytes(replies.at[pl.ds(0, slots - CAP)], reply_sem.at[1])
    emb[...] = mm(take, replies[...])

    def exchange(step, source, landing, peer):
        return remote(
            source.at[peer],
            landing.at[me],
            nss.at[step, peer],
            nrs.at[step, me],
            {"narrow": peer},
        )

    def arrive(step, landing, peer):
        wait_bytes(landing.at[peer], nrs.at[step, peer])

    def sent(step, source):
        def one(k):
            peer = lax.rem(me + k, n)
            wait_bytes(source.at[peer], nss.at[step, peer])

        return lambda: each(1, n, one)

    emb_t = jnp.transpose(emb[...])
    center = emb_t - jnp.mean(emb_t, axis=0, keepdims=True)
    inverse1 = lax.rsqrt(jnp.mean(center * center, axis=0, keepdims=True) + EPS)
    normed = center * inverse1
    normed1[...] = normed
    normed_b = normed.astype(BF16)
    for c in range(att // chunk, total_w // chunk):
        hid[c * chunk : (c + 1) * chunk, :] = mm(wt[c * chunk : (c + 1) * chunk, :], normed_b)

    near = [me, chip * 2 + 1 - core]
    near += [ys[dy] * 2 + c for dy in (1, 3) for c in (core, 1 - core)]
    near += [ys[2] * 2 + c for c in (core, 1 - core)]

    for peer in near[1:]:
        base = pl.multiple_of(att + 3 * HD * peer, HD)
        qk_out[peer] = silu(hid[pl.ds(base + HD, 2 * HD), :]).astype(BF16)
        exchange(0, qk_out, qk, peer).start()
    for peer in near[1:]:
        base = pl.multiple_of(att + 3 * HD * peer, HD)
        v_out[peer] = hid[pl.ds(base, HD), :].astype(BF16)
        exchange(4, v_out, v_in, peer).start()
    finish.append(sent(0, qk_out))
    finish.append(sent(4, v_out))
    base = pl.multiple_of(att + 3 * HD * me, HD)
    qk[me] = silu(hid[pl.ds(base + HD, 2 * HD), :]).astype(BF16)
    v_in[me] = hid[pl.ds(base, HD), :].astype(BF16)

    for c in range(att // chunk):
        hid[c * chunk : (c + 1) * chunk, :] = mm(wt[c * chunk : (c + 1) * chunk, :], normed_b)
    gate = hid[:att, :]
    gates[...] = silu(gate).astype(BF16).astype(F32)
    gn[...] = gm[...] * gates[...]
    gu[...] = silu_slope(gate)

    scale = HD**-0.5
    causal = iota((tokens, tokens), 0) <= iota((tokens, tokens), 1)

    def tri(j, i):
        return i * (i + 1) // 2 + j

    def weigh(j, i, diagonal):
        score = mm(keys[j], qk[i, :HD, :] * (0.5 * scale))
        twice = 1.0 + jnp.tanh(score)
        weight = score * twice
        slope = twice + weight * (2.0 - twice)
        if diagonal:
            weight = jnp.where(causal, weight, 0.0)
            slope = jnp.where(causal, slope, 0.0)
        wts[tri(j, i)] = weight.astype(BF16)
        slopes[tri(j, i)] = slope.astype(BF16)

    for at, here in enumerate(near):
        if at:
            arrive(0, qk, here)
        keys[here] = jnp.transpose(qk[here, HD:, :].astype(F32)).astype(BF16)
        for other in near[:at]:
            later = (here + n - other) // n
            weigh(here + later * (other - here), other + later * (here - other), False)
        weigh(here, here, True)

    def send_block(step, source, landing, i):
        @pl.when(i != me)
        def _():
            exchange(step, source, landing, i).start()

        @pl.when(i == me)
        def _():
            landing[i] = source[i]

    each(1, n, lambda k: arrive(4, v_in, lax.rem(me + k, n)))
    for i in reversed(range(n)):
        attended = jnp.zeros((HD, tokens), F32)
        for j in range(i + 1):
            attended = attended + mm(v_in[j], wts[tri(j, i)])
        heads_out[i] = attended.astype(BF16)
        send_block(1, heads_out, heads, i)
    for b in range(n):
        vals[b] = jnp.transpose(v_in[b].astype(F32)).astype(BF16)

    finish.append(sent(1, heads_out))
    each(1, n, lambda k: arrive(1, heads, lax.rem(me + k, n)))

    merged = heads[...].astype(F32).reshape(att, tokens)
    center = merged - jnp.mean(merged, axis=0, keepdims=True)
    inverse2 = lax.rsqrt(jnp.mean(center * center, axis=0, keepdims=True) + EPS)
    normed2 = center * inverse2
    grad_att = norm_back(gn[...], normed2, inverse2).astype(BF16)
    gatt_out[...] = grad_att.reshape(n, HD, tokens)
    each(1, n, lambda k: exchange(2, gatt_out, gatt, lax.rem(me + k, n)).start())
    finish.append(sent(2, gatt_out))
    gatt[me] = gatt_out[me]
    mixed = jnp.transpose(normed2 * gates[...]).astype(BF16)
    result = emb[...] + mm(mixed, wo_ref[...])
    out_ref[...] = jnp.where(live, result, 0.0).astype(BF16)
    gh[:att, :] = (gm[...] * normed2 * gu[...]).astype(BF16)
    dk[...] = jnp.zeros_like(dk)
    dv[...] = jnp.zeros_like(dv)

    for i in reversed(range(n)):

        @pl.when(i != me)
        def _():
            arrive(2, gatt, i)

        grad = gatt[i]
        query = qk[i, :HD, :]
        dq = jnp.zeros((HD, tokens), F32)
        for j in range(i + 1):
            dw = mm(vals[j], grad)
            ds = (dw * slopes[tri(j, i)].astype(F32)).astype(BF16)
            dv[j] += mm(grad, wts[tri(j, i)], NT)
            dk[j] += mm(query, ds, NT)
            dq = dq + mm(qk[j, HD:, :], ds)
        back_out[i, :HD, :] = dv[i].astype(BF16)
        back_out[i, HD : 2 * HD, :] = (dq * (0.5 * scale)).astype(BF16)
        back_out[i, 2 * HD :, :] = (dk[i] * (0.5 * scale)).astype(BF16)
        send_block(3, back_out, back, i)

    finish.append(sent(3, back_out))
    hid[att:, :] = silu_slope(hid[att:, :])
    put = onehot(iota((slots, tokens), 0) == target)
    gate_part = mm(w_ref[:, :att], gh[:att, :])
    each(1, n, lambda k: arrive(3, back, lax.rem(me + k, n)))
    for h in range(HEADS):
        base = att + 3 * HD * h
        gh[base : base + HD, :] = back[h, :HD, :]
        gh[base + HD : base + 3 * HD, :] = (
            back[h, HD:, :].astype(F32) * hid[base + HD : base + 3 * HD, :]
        ).astype(BF16)
    grad_norm1 = gate_part + mm(w_ref[:, att:], gh[att:, :])
    grad_emb = norm_back(grad_norm1, normed1[...], inverse1) + up_t[...]
    ge[...] = jnp.where(live_t, grad_emb, 0.0).astype(BF16)

    own = tile16(chip * slots + wide * CAP)

    for dy in DY:
        y = ys[dy]
        block = ge[pl.ds(pl.multiple_of(y * cols, cols), cols), :]
        outgoing[pl.ds(pl.multiple_of(y * slots, slots), slots), :] = mm(put, block, NT).astype(BF16)
        for dz, dx in AROUND:
            if dz or dx or dy:
                o = far(dz, dx)
                remote(
                    outgoing.at[tile16(y * slots + o * CAP)],
                    arriving.at[own],
                    give_sem.at[0],
                    give_sem.at[1],
                    {"wide": o, "narrow": y * 2 + core},
                ).start()
    for wait in finish:
        wait()
    finish.clear()
    finish.append(lambda: wait_bytes(outgoing.at[pl.ds(0, chips * slots - CAP)], give_sem.at[0]))
    arriving[own, :] = outgoing[own, :]
    wait_bytes(arriving.at[pl.ds(0, chips * slots - CAP)], give_sem.at[1])

    half_rows = rows_dev // 2
    parts = 4
    piece = half_rows // parts
    sibling = {"narrow": chip * 2 + 1 - core}

    def rows_at(side, p):
        return pl.ds(pl.multiple_of(side * half_rows + p * piece, piece), piece)

    def swap(p):
        return remote(sib_out.at[p], sib_in.at[p], sib_ss.at[p], sib_rs.at[p], sibling)

    def ring(way, hop, p):
        spot = sum_ref.at[ys[(1 - hop) * way % chips], rows_at(core, p)]
        lane = 2 * hop - 2 + (way < 0)
        return remote(
            spot, spot, ring_ss.at[lane, p], ring_rs.at[lane, p], {"narrow": ys[way % chips] * 2 + core}
        )

    def pass_on(k, p):
        spot = sum_ref.at[ys[k], rows_at(core, p)]
        return remote(spot, spot, pass_ss.at[k, p], pass_rs.at[k, p], sibling)

    groups = piece // 128

    def update(side, p):
        first = side * (half_rows // 128) + p * groups
        for g in range(groups):
            part = pl.ds(pl.multiple_of(side * half_rows + p * piece + g * 128, 128), 128)
            grads = [sum_ref[y, part, :].astype(F32) for y in range(chips)]
            square = sum(v * v for v in grads)
            mean = jnp.sum(square, axis=1, keepdims=True) * (1.0 / width)
            line = jnp.transpose(jnp.broadcast_to(mean, (128, 128)))[:1, :]
            spot = pl.ds(first + g, 1)
            accum = accum_ref[spot, :] + line
            new_accum_ref[spot, :] = accum
            factor = jnp.transpose(jnp.broadcast_to(RATE * lax.rsqrt(accum), (128, 128)))
            for y in range(chips):
                lane = slice(y * cols, (y + 1) * cols)
                new_table_ref[part, lane] = tab[part, lane] - grads[y] * factor

    low, high = tuple(range(parts // 2)), tuple(range(parts // 2, parts))
    order = [p for pair in zip(low, high) for p in pair]

    def offer(p):
        sib_out[p] = mm(hot[rows_at(1 - core, p), :], arriving[...]).astype(BF16)
        swap(p).start()

    offer(order[0])
    for at, p in enumerate(order):
        if at + 1 < parts:
            offer(order[at + 1])
        total = mm(hot[rows_at(core, p), :], arriving[...])
        swap(p).wait_recv()
        sum_ref[chip, rows_at(core, p), :] = (total + sib_in[p].astype(F32)).astype(BF16)
        ring(1 if p in low else -1, 1, p).start()
        pass_on(0, p).start()
    for p in order:
        ring(-1 if p in low else 1, 1, p).start()
    for p in order:
        way = 1 if p in low else -1
        ring(way, 1, p).wait_recv()
        ring(way, 2, p).start()
        pass_on(-way % chips, p).start()
    for at, p in enumerate(order):
        way = 1 if p in low else -1
        ring(-way, 1, p).wait_recv()
        pass_on(way % chips, p).start()
    for at, p in enumerate(order):
        way = 1 if p in low else -1
        ring(way, 2, p).wait_recv()
        pass_on(2, p).start()
        update(core, p)
        if at:
            q = order[at - 1]
            for k in range(chips):
                pass_on(k, q).wait_recv()
            update(1 - core, q)
    for k in range(chips):
        pass_on(k, order[-1]).wait_recv()
    update(1 - core, order[-1])

    for wait in finish:
        wait()
    for p in range(parts):
        swap(p).wait_send()
        for way in (1, -1):
            ring(way, 1, p).wait_send()
        ring(1 if p in low else -1, 2, p).wait_send()
        for k in range(chips):
            pass_on(k, p).wait_send()


def run_step(n_wide, n, table, accum, ids, lengths, w_uvqk, w_out, cotangent):
    rows_dev, width = table.shape
    tokens = ids.shape[1]
    att = HEADS * HD
    chips = n // 2
    slots = n_wide * CAP
    cols = width // chips
    parts = 4
    vmem = pl.BlockSpec(memory_space=pltpu.VMEM)
    hbm = pl.BlockSpec(memory_space=pltpu.HBM)
    dma = pltpu.SemaphoreType.DMA
    return pl.pallas_call(
        functools.partial(step_kernel, n_wide, n),
        out_shape=(
            pltpu.VMEM((tokens, width), BF16),
            pltpu.VMEM((rows_dev, width), F32),
            pltpu.VMEM((rows_dev // 128, 128), F32),
        ),
        in_specs=[hbm, vmem, vmem, pl.BlockSpec(memory_space=pltpu.SMEM), hbm, hbm, hbm],
        out_specs=(vmem, vmem, vmem),
        scratch_shapes=[
            pltpu.VMEM((chips, rows_dev, cols), BF16),
            pltpu.VMEM((rows_dev, width), F32),
            pltpu.VMEM(w_uvqk.shape, BF16),
            pltpu.VMEM(w_out.shape, BF16),
            pltpu.VMEM((tokens, width), BF16),
            pltpu.VMEM((w_uvqk.shape[1], width), BF16),
            pltpu.VMEM((n_wide, 1, 128), jnp.int32),
            pltpu.VMEM((n_wide, 1, 128), jnp.int32),
            pltpu.VMEM((slots, width), BF16),
            pltpu.VMEM((slots, width), BF16),
            pltpu.VMEM((chips, n_wide // 8, 128), jnp.int32),
            pltpu.VMEM((rows_dev, chips * slots), BF16),
            pltpu.VMEM((tokens, width), F32),
            pltpu.VMEM((4 * att, tokens), F32),
            pltpu.VMEM((width, tokens), F32),
            pltpu.VMEM((n, 2 * HD, tokens), BF16),
            pltpu.VMEM((n, 2 * HD, tokens), BF16),
            pltpu.VMEM((n, HD, tokens), BF16),
            pltpu.VMEM((n, HD, tokens), BF16),
            pltpu.VMEM((n, tokens, HD), BF16),
            pltpu.VMEM((n, tokens, HD), BF16),
            pltpu.VMEM((n * (n + 1) // 2, tokens, tokens), BF16),
            pltpu.VMEM((n * (n + 1) // 2, tokens, tokens), BF16),
            pltpu.VMEM((n, HD, tokens), BF16),
            pltpu.VMEM((n, HD, tokens), BF16),
            pltpu.VMEM((att, tokens), F32),
            pltpu.VMEM((att, tokens), F32),
            pltpu.VMEM((att, tokens), F32),
            pltpu.VMEM((att, tokens), F32),
            pltpu.VMEM((n, HD, tokens), BF16),
            pltpu.VMEM((n, HD, tokens), BF16),
            pltpu.VMEM((n, HD, tokens), F32),
            pltpu.VMEM((n, HD, tokens), F32),
            pltpu.VMEM((n, 3 * HD, tokens), BF16),
            pltpu.VMEM((n, 3 * HD, tokens), BF16),
            pltpu.VMEM((4 * att, tokens), BF16),
            pltpu.VMEM((width, tokens), F32),
            pltpu.VMEM((width, tokens), BF16),
            pltpu.VMEM((chips * slots, cols), BF16),
            pltpu.VMEM((chips * slots, cols), BF16),
            pltpu.VMEM((parts, rows_dev // 2 // parts, cols), BF16),
            pltpu.VMEM((parts, rows_dev // 2 // parts, cols), BF16),
            dma((4,)),
            dma((2,)),
            dma((2,)),
            dma((2,)),
            dma((5, n)),
            dma((5, n)),
            dma((2,)),
            dma((parts,)),
            dma((parts,)),
            dma((4, parts)),
            dma((4, parts)),
            dma((chips, parts)),
            dma((chips, parts)),
        ],
        compiler_params=pltpu.CompilerParams(
            collective_id=0, has_side_effects=True, vmem_limit_bytes=52 * MIB
        ),
    )(table, accum, ids, lengths, w_uvqk, w_out, cotangent)


def local(table, accum, ids, lengths, w_uvqk, w_out, cotangent):
    n_wide = lax.axis_size("wide")
    n_narrow = lax.axis_size("narrow")
    width = table.shape[1]
    tokens = ids.shape[1]
    output, new_table, new_accum = run_step(
        n_wide,
        n_narrow,
        table,
        accum.reshape(-1, 128),
        ids,
        lengths,
        w_uvqk,
        w_out,
        cotangent.reshape(tokens, width),
    )
    return (output.reshape(1, tokens, width), new_table, new_accum.reshape(accum.shape))


def solution(mesh):
    in_specs = (
        P("wide", None),
        P("wide"),
        P("wide", "narrow"),
        P("wide"),
        P(),
        P(),
        P("wide", "narrow", None),
    )
    out_specs = (P("wide", "narrow", None), P("wide", None), P("wide"))
    return jax.shard_map(local, mesh=mesh, in_specs=in_specs, out_specs=out_specs, check_vma=False)
```
